128 devices in a mesh: seq: 32 (over x, z, core), exp: 4 (over y).
Axes of the slice: x: 4, y: 4, z: 4, core: 2. Of those that a mesh axis runs over, the one named last changes fastest.
Arguments:
- coarse_in: bfloat16 [4096, 1024], P('seq', 'exp'), may hold values from -24 to 24
- norm1_gain: float32 [1024], replicated, may hold values from 0.1 to 1.9
- qkv_weight: bfloat16 [3, 1024, 1024], P(None, None, 'exp'), may hold values from -0.1875 to 0.1875
- head_scale: float32 [16], P('exp'), may hold values from 2.5 to 40, as said below
- out_weight: bfloat16 [1024, 1024], P('exp'), may hold values from -0.1875 to 0.1875
- norm2_gain: float32 [1024], replicated, may hold values from 0.1 to 1.9
- mlp_in: bfloat16 [1024, 4096], P(None, 'exp'), may hold values from -0.1875 to 0.1875
- mlp_out: bfloat16 [4096, 1024], P('exp'), may hold values from -0.09375 to 0.09375
- fine_in: bfloat16 [20480, 1024], P(('seq', 'exp')), may hold values from -24 to 24
- parent_device: int32 [20480, 1], P(('seq', 'exp')), may hold values from 0 to 31; in each aligned block of 160 rows (0 to 159, 160 to 319, ...) at most 10 rows name the same one
- parent_row: int32 [20480], P(('seq', 'exp')), may hold values from 0 to 127
- octant: int32 [20480], P(('seq', 'exp')), may hold values from 0 to 7
- octant_table: bfloat16 [8, 1024], replicated, may hold values from -6 to 6
- norm3_gain: float32 [1024], replicated, may hold values from 0.1 to 1.9
- expert_ids: int32 [20480, 2], P(('seq', 'exp')), may hold values from 0 to 15, all different within a row; in each aligned block of 160 rows (0 to 159, 160 to 319, ...) at most 30 rows name the same one
- expert_gates: float32 [20480, 2], P(('seq', 'exp')), may hold values from 0.2 to 1
- gate_weight: bfloat16 [32, 1024, 2048], P('seq', None, 'exp'), may hold values from -0.1875 to 0.1875
- up_weight: bfloat16 [32, 1024, 2048], P('seq', None, 'exp'), may hold values from -0.1875 to 0.1875
- down_weight: bfloat16 [32, 1024, 2048], P('seq', None, 'exp'), may hold values from -0.09375 to 0.09375
Outputs:
- coarse_out: bfloat16 [4096, 1024], P('seq')
- fine_out: bfloat16 [20480, 1024], P(('seq', 'exp'))
The draws below stay inside these ranges and needn't reach their ends.
Inputs may be any that keep to these rules, and one draw needn't show every extreme that they name: `parent_device`: among the rows of one device no index appears more than 10 times. `expert_ids`: each row names two different experts; among the rows of one device no expert appears more than 30 times. `head_scale`: one positive scale for each head.
All inputs are finite; a program needn't handle non-finite values.
Results may differ from the reference program's by a relative error of at most 0.0095.
Values may be sent and summed in bfloat16 or wider, within the bound.
No kernel may reach another device: no remote copies, remote signals or barrier semaphores. Data moves between devices by JAX's collectives and lax.ppermute only.
A program may use at most 128 MiB of HBM per device.

```python
import math
import jax
import jax.numpy as jnp
import numpy as np
from jax import lax

D = 1024
HEADS = 16
HEAD_DIM = 64
MLP_FF = 4096
EXPERTS = 16
FF = 4096
CT_DEV = 128
FT_DEV = 160
CAP = 30
PCAP = 10
CTOK = 4096
FTOK = 20480
N_SEQ = 32
DEVICES = 128


def scaled_rows(key, rows, cols, block, tight_even, tight_odd):
    first = jax.random.fold_in(key, 0)
    second = jax.random.fold_in(key, 1)
    third = jax.random.fold_in(key, 2)
    fifth = jax.random.fold_in(key, 4)
    sixth = jax.random.fold_in(key, 5)
    base = jnp.clip(jax.random.normal(first, (rows, cols), jnp.float32), -4.0, 4.0)
    spread = 1.15
    table = jnp.clip(jax.random.normal(fifth, (32, cols), jnp.float32), -3.0, 3.0)
    parity = jnp.arange(rows, dtype=jnp.int32) // block % 2
    pick = jax.random.randint(sixth, (rows,), 0, 16, dtype=jnp.int32) + 16 * parity
    tight = jnp.where(parity == 1, tight_odd, tight_even).astype(jnp.float32)[:, None]
    mixture = tight * table[pick] + jnp.sqrt(1.0 - tight * tight) * base
    row_scale = jnp.exp(jax.random.uniform(second, (rows, 1), jnp.float32, -spread, spread))
    col_scale = jnp.exp(jax.random.uniform(third, (1, cols), jnp.float32, -spread, spread))
    return jnp.clip(mixture * row_scale * col_scale, -24.0, 24.0)


def draw_coarse_in(key, part):
    return scaled_rows(jax.random.fold_in(key, 11), CTOK, D, CT_DEV, 0.8, 0.93).astype(jnp.bfloat16)


def draw_fine_in(key, part):
    return scaled_rows(jax.random.fold_in(key, 23), FTOK, D, FT_DEV, 0.0, 0.0).astype(jnp.bfloat16)


def draw_head_scale(key, part):
    key = jax.random.fold_in(key, 37)
    return jnp.exp(jax.random.uniform(key, (HEADS,), jnp.float32, math.log(2.5), math.log(6.0)))


def plant(entries, rng, smallest, high):
    dims = entries.shape
    spot = [jax.random.randint(jax.random.fold_in(rng, axis), (), 0, dims[axis]) for axis in range(len(dims))]
    entries = entries.at[tuple(spot)].set(smallest)
    longest = dims.index(max(dims))
    spot[longest] = (spot[longest] + 1) % dims[longest]
    return entries.at[tuple(spot)].set(high)


def steps_of(own_key, shape, pieces, least, high):
    def one(dim, blocks):
        draws = jax.random.uniform(jax.random.fold_in(jax.random.fold_in(own_key, 6), dim), (blocks,), jnp.float32, least / len(pieces), high / len(pieces))
        return jnp.repeat(jnp.exp(draws), shape[dim] // blocks).reshape((-1,) + (1,) * (len(shape) - dim - 1))

    loudness = one(*pieces[0])
    for cut in pieces[1:]:
        loudness = loudness * one(*cut)
    return loudness


def shared_out(stream_key, own, number, rows, amount, top, limit, skew):
    ranking = jax.random.permutation(stream_key, amount)
    heavy_load, usual = shares(amount, rows * top, limit, skew, True), shares(amount, rows * top, limit, skew, False)
    places = jnp.arange(amount)

    def named(sizes, offset_by):
        used = int((sizes > 0).sum())
        fixed = max(1, used // 4)
        passed = fixed + (places - fixed + offset_by * (used - fixed)) % max(1, amount - fixed)
        return jnp.zeros((amount,), jnp.int32).at[ranking[jnp.where(places < fixed, places, passed)]].set(jnp.asarray(sizes, jnp.int32))

    sizes = jnp.where(number % 4 == 0, named(heavy_load, number // 4), named(usual, number - number // 4 - 1))
    mixed = jax.random.permutation(jax.random.fold_in(own, 3), amount)
    giver, sink = mixed[0:amount // 2 * 2:2], mixed[1:amount // 2 * 2:2]
    margin = jnp.minimum(sizes[giver] - 1, limit - sizes[sink]) // 2
    margin = jnp.where((giver == ranking[0]) | (sink == ranking[0]) | (sizes[sink] == 0), 0, jnp.maximum(margin, 0))
    passed = jax.random.randint(jax.random.fold_in(own, 4), (amount // 2,), 0, 1 << 20) % (margin + 1)
    sizes = sizes.at[giver].add(-passed).at[sink].add(passed)
    members = jnp.searchsorted(jnp.cumsum(sizes), jnp.arange(rows * top), side="right").astype(jnp.int32)
    grid = members.reshape(top, rows).T
    grid = grid[jax.random.permutation(jax.random.fold_in(own, 1), rows)]
    offset_by = jax.random.randint(jax.random.fold_in(own, 2), (rows, 1), 0, top)
    return jnp.take_along_axis(grid, (jnp.arange(top)[None, :] + offset_by) % top, axis=1)


def shares(number_of, total, reach, slope, full):
    weights = [(1 << 20) // math.isqrt(standing ** slope) + 1 for standing in range(1, number_of + 1)]
    largest = reach if full else min(reach, max(-(-total // number_of), total * weights[0] // sum(weights)))
    least = 1 if total - largest >= number_of - 1 else 0
    given, spare = [largest] + [least] * (number_of - 1), total - largest - least * (number_of - 1)
    while spare > 0:
        candidates = [i for i in range(1, number_of) if given[i] < largest] or [i for i in range(1, number_of) if given[i] < reach]
        mass, budget = sum([weights[i] for i in candidates]), spare
        for i in candidates:
            extra = min(reach - given[i], max(1, budget * weights[i] // mass), spare)
            given[i] = given[i] + extra
            spare = spare - extra
    return np.array(given)


def bell_draw(stream_key, dims, scale, limit, shards=(), kind=jnp.bfloat16):
    drawn = scale * jax.random.normal(stream_key, dims, jnp.float32)
    if shards:
        drawn = drawn * steps_of(stream_key, dims, shards, -0.22, 0.18)
    return jnp.clip(drawn, -limit, limit).astype(kind)


def setup_inputs(seed: int = 0) -> dict:
    key_of = jax.random.split(jax.random.key(seed), 20)
    coarse_in = draw_coarse_in(jax.random.fold_in(key_of[19], 71), 0)
    norm1_gain = jnp.clip(1.0 + 0.18 * jax.random.normal(key_of[1], (D,), jnp.float32), 0.1, 1.9)
    qkv_weight = bell_draw(key_of[2], (3, D, D), D ** -0.5, 0.1875, ((2, 4),))
    head_scale = draw_head_scale(jax.random.fold_in(key_of[19], 71), 0)
    out_weight = bell_draw(key_of[4], (D, D), D ** -0.5, 0.1875, ((0, 4),))
    norm2_gain = jnp.clip(1.0 + 0.18 * jax.random.normal(key_of[5], (D,), jnp.float32), 0.1, 1.9)
    mlp_in = bell_draw(key_of[6], (D, MLP_FF), D ** -0.5, 0.1875, ((1, 4),))
    mlp_out = bell_draw(key_of[7], (MLP_FF, D), MLP_FF ** -0.5, 0.09375, ((0, 4),))
    fine_in = draw_fine_in(jax.random.fold_in(key_of[19], 71), 0)
    parent_device_keys = jax.random.split(jax.random.fold_in(key_of[9], 1), FTOK // FT_DEV)
    parent_device_turns = jax.random.permutation(jax.random.fold_in(key_of[9], 3), FTOK // FT_DEV)
    parent_device = jax.vmap(lambda own, number: shared_out(jax.random.fold_in(key_of[9], 2), own, number, FT_DEV, N_SEQ, 1, PCAP, 1))(parent_device_keys, parent_device_turns).reshape((FTOK, 1))
    parent_row = plant(jax.random.randint(key_of[10], (FTOK,), 0, CT_DEV), jax.random.fold_in(key_of[10], 1), 0, CT_DEV - 1).astype(jnp.int32)
    octant = plant(jax.random.randint(key_of[11], (FTOK,), 0, 8), jax.random.fold_in(key_of[11], 1), 0, 7).astype(jnp.int32)
    octant_table = bell_draw(key_of[12], (8, D), 1.0, 6.0)
    norm3_gain = jnp.clip(1.0 + 0.18 * jax.random.normal(key_of[13], (D,), jnp.float32), 0.1, 1.9)
    expert_ids_keys = jax.random.split(jax.random.fold_in(key_of[14], 1), FTOK // FT_DEV)
    expert_ids_turns = jax.random.permutation(jax.random.fold_in(key_of[14], 3), FTOK // FT_DEV)
    expert_ids = jax.vmap(lambda own, number: shared_out(jax.random.fold_in(key_of[14], 2), own, number, FT_DEV, EXPERTS, 2, CAP, 2))(expert_ids_keys, expert_ids_turns).reshape((FTOK, 2))
    expert_gates = jnp.clip(0.2 + 0.8 * jax.random.uniform(key_of[15], (FTOK, 2), jnp.float32) ** steps_of(key_of[15], (FTOK, 2), ((0, 128),), -0.2, 0.2), 0.2, 1.0)
    gate_weight = bell_draw(key_of[16], (2 * EXPERTS, D, FF // 2), D ** -0.5, 0.1875, ((0, 32), (2, 4)))
    up_weight = bell_draw(key_of[17], (2 * EXPERTS, D, FF // 2), D ** -0.5, 0.1875, ((0, 32), (2, 4)))
    down_weight = bell_draw(key_of[18], (2 * EXPERTS, D, FF // 2), FF ** -0.5, 0.09375, ((0, 32), (2, 4)))
    return {"coarse_in": coarse_in, "norm1_gain": norm1_gain, "qkv_weight": qkv_weight, "head_scale": head_scale, "out_weight": out_weight, "norm2_gain": norm2_gain, "mlp_in": mlp_in, "mlp_out": mlp_out, "fine_in": fine_in, "parent_device": parent_device, "parent_row": parent_row, "octant": octant, "octant_table": octant_table, "norm3_gain": norm3_gain, "expert_ids": expert_ids, "expert_gates": expert_gates, "gate_weight": gate_weight, "up_weight": up_weight, "down_weight": down_weight}


EPSILON = 1e-06

def rms_scale(vector_in, gain_vec):
    return vector_in * lax.rsqrt(lax.optimization_barrier(jnp.mean(vector_in * vector_in, axis=-1, keepdims=True)) + EPSILON) * gain_vec

def head_norm(projection):
    shaped = projection.reshape(CTOK, HEADS, HEAD_DIM)
    return (shaped * lax.rsqrt(lax.optimization_barrier(jnp.mean(shaped * shaped, axis=-1, keepdims=True)) + EPSILON)).astype(jnp.bfloat16)

def reference(coarse_in, norm1_gain, qkv_weight, head_scale, out_weight, norm2_gain, mlp_in, mlp_out, fine_in, parent_device, parent_row, octant, octant_table, norm3_gain, expert_ids, expert_gates, gate_weight, up_weight, down_weight):
    residual = coarse_in.astype(jnp.float32)
    normed = rms_scale(residual, norm1_gain).astype(jnp.bfloat16)
    queries = head_norm(jnp.dot(normed, qkv_weight[0], preferred_element_type=jnp.float32))
    key_heads = head_norm(jnp.dot(normed, qkv_weight[1], preferred_element_type=jnp.float32))
    value_heads = jnp.dot(normed, qkv_weight[2], preferred_element_type=jnp.float32).astype(jnp.bfloat16).reshape(CTOK, HEADS, HEAD_DIM)
    factor = head_scale / math.sqrt(HEAD_DIM)

    def one_head(head_index):
        query_head = lax.dynamic_index_in_dim(queries, head_index, 1, keepdims=False)
        key_head = lax.dynamic_index_in_dim(key_heads, head_index, 1, keepdims=False)
        value_head = lax.dynamic_index_in_dim(value_heads, head_index, 1, keepdims=False)
        scale_now = factor[head_index]

        def one_block(query_block):
            scores = jnp.dot(query_block, key_head.T, preferred_element_type=jnp.float32) * scale_now
            row_top = lax.optimization_barrier(jnp.max(scores, axis=-1, keepdims=True))
            weights = jnp.exp(scores - row_top)
            running = lax.optimization_barrier(jnp.sum(weights, axis=-1, keepdims=True))
            return jnp.dot(weights.astype(jnp.bfloat16), value_head, preferred_element_type=jnp.float32) / running
        blocks = lax.map(one_block, query_head.reshape(N_SEQ, CT_DEV, HEAD_DIM))
        return blocks.reshape(CTOK, HEAD_DIM)
    heads_out = lax.map(one_head, jnp.arange(HEADS, dtype=jnp.int32))
    attended = jnp.transpose(heads_out, (1, 0, 2)).reshape(CTOK, D).astype(jnp.bfloat16)
    mixed_sum = residual + jnp.dot(attended, out_weight, preferred_element_type=jnp.float32)
    normed2 = rms_scale(mixed_sum, norm2_gain).astype(jnp.bfloat16)
    inner_coarse = jax.nn.gelu(jnp.dot(normed2, mlp_in, preferred_element_type=jnp.float32)).astype(jnp.bfloat16)
    coarse_out = (mixed_sum + jnp.dot(inner_coarse, mlp_out, preferred_element_type=jnp.float32)).astype(jnp.bfloat16)
    parent_index = (parent_device[:, 0] * CT_DEV + parent_row).astype(jnp.int32)
    parents = coarse_out[parent_index].astype(jnp.float32)
    fine_sum = fine_in.astype(jnp.float32) + parents + octant_table[octant].astype(jnp.float32)
    fine_norm = rms_scale(fine_sum, norm3_gain).astype(jnp.bfloat16)
    grouped_ids = expert_ids.reshape(DEVICES, 2 * FT_DEV)
    member = (grouped_ids[:, :, None] == jnp.arange(EXPERTS, dtype=jnp.int32)[None, None, :]).astype(jnp.int32)
    expert_slot = lax.optimization_barrier(jnp.sum(member * (jnp.cumsum(member, axis=1) - 1), axis=-1))
    position = (jnp.arange(DEVICES, dtype=jnp.int32)[:, None] * CAP + expert_slot).reshape(-1).astype(jnp.int32)
    flat_ids = grouped_ids.reshape(-1).astype(jnp.int32)
    token_of = (jnp.arange(2 * FTOK, dtype=jnp.int32) // 2).astype(jnp.int32)
    buffer_rows = jnp.zeros((EXPERTS, DEVICES * CAP, D), jnp.bfloat16).at[flat_ids, position].set(fine_norm[token_of])

    def run_expert(expert_index):
        rows_in = lax.dynamic_index_in_dim(buffer_rows, expert_index, 0, keepdims=False)
        running = jnp.zeros((DEVICES * CAP, D), jnp.float32)
        for half in range(2):
            which = 2 * expert_index + half
            gate_half = lax.dynamic_index_in_dim(gate_weight, which, 0, keepdims=False)
            up_half = lax.dynamic_index_in_dim(up_weight, which, 0, keepdims=False)
            down_half = lax.dynamic_index_in_dim(down_weight, which, 0, keepdims=False)
            gate_part = jnp.dot(rows_in, gate_half, preferred_element_type=jnp.float32)
            up_part = jnp.dot(rows_in, up_half, preferred_element_type=jnp.float32)
            inner_act = (jax.nn.silu(gate_part) * up_part).astype(jnp.bfloat16)
            running = running + jnp.dot(inner_act, down_half.T, preferred_element_type=jnp.float32)
        return running
    expert_out = lax.map(run_expert, jnp.arange(EXPERTS, dtype=jnp.int32))
    picked = expert_out[flat_ids, position]
    expert_mix = lax.optimization_barrier(jnp.sum(picked.reshape(FTOK, 2, D) * expert_gates[:, :, None], axis=1))
    fine_out = (fine_sum + expert_mix).astype(jnp.bfloat16)
    return (coarse_out, fine_out)
```

```python
import math

import jax
import jax.numpy as jnp
from jax import lax
from jax.experimental import pallas as pl
from jax.experimental.pallas import tpu as pltpu
from jax.sharding import PartitionSpec as P

EPSILON = 1e-06
BF = jnp.bfloat16
F32 = jnp.float32
VMEM = 56 * 1024 * 1024

N_SEQ = 32
N_EXP = 4
ROWS = 128
D = 1024
HEADS = 4
HD = 64
FINE = 160
EXPERTS = 16
SLOTS = 32
PSLOTS = 16
QUADS = [[4 * a + b for b in range(4)] for a in range(8)]
SWAP = [(i, i ^ 1) for i in range(N_SEQ)]


def call(kernel, out_shape, *args, flops=0, nbytes=0, smem=(), **kw):
    space = [
        pl.BlockSpec(memory_space=pltpu.SMEM if i in smem else pltpu.VMEM) for i in range(len(args))
    ]
    outs = jax.tree.map(lambda _: pl.BlockSpec(memory_space=pltpu.VMEM), out_shape)
    return pl.pallas_call(
        kernel,
        out_shape=out_shape,
        in_specs=space,
        out_specs=outs,
        compiler_params=pltpu.CompilerParams(vmem_limit_bytes=VMEM),
        cost_estimate=pl.CostEstimate(flops=flops, bytes_accessed=nbytes, transcendentals=0),
        **kw,
    )(*args)


def sds(shape, dtype):
    return jax.ShapeDtypeStruct(shape, dtype)


def dot(a, b):
    return jnp.dot(a, b, preferred_element_type=F32)


def dot_nt(a, b):
    return lax.dot_general(a, b, (((1,), (1,)), ((), ())), preferred_element_type=F32)


def iota(shape, dim):
    return lax.broadcasted_iota(jnp.int32, shape, dim)


def rms(x, gain):
    return x * lax.rsqrt(jnp.mean(x * x, axis=-1, keepdims=True) + EPSILON) * gain


def hot(cond):
    return jnp.where(cond, 1.0, 0.0).astype(BF)


def route_kernel(pd_ref, pdt_ref, prow_ref, ids_ref, idst_ref, pidx_ref, didx_ref, didxt_ref, req_ref):
    before = hot(iota((FINE, FINE), 0) > iota((FINE, FINE), 1))
    beforet = hot(iota((FINE, FINE), 0) < iota((FINE, FINE), 1))
    pd, pdt = pd_ref[...], pdt_ref[...]
    member = hot(pd == iota((FINE, N_SEQ), 1))
    rank = jnp.sum(member.astype(F32) * dot(before, member), axis=1, keepdims=True)
    pidx_ref[...] = pd * PSLOTS + rank.astype(jnp.int32)
    membert = hot(pdt == iota((N_SEQ, FINE), 0))
    rankt = jnp.sum(membert.astype(F32) * dot(membert, beforet), axis=0, keepdims=True)
    pidxt = pdt * PSLOTS + rankt.astype(jnp.int32)
    wanted = hot(pidxt == iota((N_SEQ * PSLOTS, FINE), 0))
    rows = jnp.broadcast_to(prow_ref[...].astype(F32), (FINE, ROWS)).astype(BF)
    req_ref[...] = dot(wanted, rows).astype(BF).reshape(N_SEQ, PSLOTS, ROWS)
    m = [hot(ids_ref[:, k : k + 1] == iota((FINE, EXPERTS), 1)) for k in range(2)]
    ahead = dot(before, m[0] + m[1])
    mt = [hot(idst_ref[k : k + 1, :] == iota((EXPERTS, FINE), 0)) for k in range(2)]
    aheadt = dot(mt[0] + mt[1], beforet)
    for k in range(2):
        r = jnp.sum(m[k].astype(F32) * ahead, axis=1, keepdims=True)
        didx_ref[:, k : k + 1] = ids_ref[:, k : k + 1] * SLOTS + r.astype(jnp.int32)
        rt = jnp.sum(mt[k].astype(F32) * aheadt, axis=0, keepdims=True)
        didxt_ref[k : k + 1, :] = idst_ref[k : k + 1, :] * SLOTS + rt.astype(jnp.int32)


def qkv_kernel(feats_ref, gain_ref, w_ref, req_ref, q_ref, kv_ref):
    x = jnp.concatenate([feats_ref[c].astype(F32) for c in range(N_EXP)], axis=1)
    normed = rms(x, gain_ref[...]).astype(BF)
    proj = [dot(normed, w_ref[i]) for i in range(3)]
    for h in range(HEADS):
        piece = [p[:, h * HD : (h + 1) * HD] for p in proj]
        q, k = [
            v * lax.rsqrt(jnp.mean(v * v, axis=-1, keepdims=True) + EPSILON) for v in piece[:2]
        ]
        q_ref[h] = jnp.concatenate([q, jnp.zeros_like(q)], axis=1).astype(BF)
        kv = jnp.concatenate([k, piece[2]], axis=1).astype(BF)
        for t in range(h, N_SEQ, HEADS):
            kv_ref[t, 0:ROWS, :] = kv
    kv_ref[:, ROWS : ROWS + PSLOTS, :] = req_ref[...]


def attn_kernel(scale_ref, q_ref, kv_ref, out_ref):
    kv = kv_ref[:, 0:ROWS, :].reshape(N_SEQ * ROWS, 2 * HD)
    vones = jnp.where(iota(kv.shape, 1) < HD, jnp.ones_like(kv), kv)
    c = scale_ref[0, 0]
    for b in range(4):
        s = dot_nt(q_ref[b], kv)
        top = jnp.max(s, axis=-1, keepdims=True)
        p = jnp.exp2((s - top) * c).astype(BF)
        o = dot(p, vones)
        out_ref[b] = (o[:, HD:] / o[:, :HD]).astype(BF)


def proj_kernel(att_ref, w_ref, out_ref):
    acc = dot(att_ref[0], w_ref[0:HD, :])
    for h in range(1, HEADS):
        acc = acc + dot(att_ref[h], w_ref[h * HD : (h + 1) * HD, :])
    out_ref[...] = acc.astype(BF)


def mixed_kernel(y_ref, parts_ref, feats_ref, gain_ref, mixed_ref, normed_ref):
    start = pl.multiple_of(y_ref[0, 0] * 32, 32)
    x = jnp.concatenate(
        [feats_ref[c, pl.ds(start, 32), :].astype(F32) for c in range(N_EXP)], axis=1
    )
    total = parts_ref[0].astype(F32)
    for c in range(1, N_EXP):
        total = total + parts_ref[c].astype(F32)
    mixed = x + total
    mixed_ref[...] = mixed
    normed_ref[...] = rms(mixed, gain_ref[...]).astype(BF)


def mlp_kernel(x_ref, win_ref, wout_ref, out_ref):
    inner = jax.nn.gelu(dot(x_ref[...], win_ref[...])).astype(BF)
    out_ref[...] = dot(inner, wout_ref[...]).astype(BF)


def coarse_kernel(parts_ref, mixed_ref, out_ref):
    total = parts_ref[0].astype(F32)
    for c in range(1, N_EXP):
        total = total + parts_ref[c].astype(F32)
    out_ref[...] = (mixed_ref[...] + total).astype(BF)


def serve_kernel(kv_ref, coarse_ref, out_ref):
    req = kv_ref[:, ROWS : ROWS + PSLOTS, :].reshape(N_SEQ * PSLOTS, ROWS)
    chosen = hot(req.astype(F32) == iota(req.shape, 1).astype(F32))
    out_ref[...] = dot(chosen, coarse_ref[...]).astype(BF)


def fine_kernel(rows_ref, pidx_ref, fine_ref, oct_ref, table_ref, gain_ref, didxt_ref, sum_ref, out_ref):
    pick = hot(pidx_ref[...] == iota((FINE, N_SEQ * PSLOTS), 1))
    parents = dot(pick, rows_ref[...])
    octs = dot(hot(oct_ref[...] == iota((FINE, 8), 1)), table_ref[...])
    fine_sum = fine_ref[...].astype(F32) + parents + octs
    sum_ref[...] = fine_sum
    normed = rms(fine_sum, gain_ref[...]).astype(BF)
    slot = iota((EXPERTS * SLOTS, FINE), 0)
    place = hot((didxt_ref[0:1, :] == slot) | (didxt_ref[1:2, :] == slot))
    out_ref[...] = dot(place, normed).astype(BF)


def ffn_kernel(x1_ref, x2_ref, gate_ref, up_ref, down_ref, o1_ref, o2_ref, a1, a2):
    j = pl.program_id(0)
    for x_ref, a in ((x1_ref, a1), (x2_ref, a2)):
        x = x_ref[...]
        g = dot(x, gate_ref[0])
        u = dot(x, up_ref[0])
        act = (0.5 * g * (1.0 + jnp.tanh(0.5 * g)) * u).astype(BF)
        part = dot_nt(act, down_ref[0])

        @pl.when(j == 0)
        def _():
            a[...] = part

        @pl.when(j > 0)
        def _():
            a[...] += part

    @pl.when(j == N_EXP - 1)
    def _():
        o1_ref[...] = a1[...]
        o2_ref[...] = a2[...].astype(BF)


def ffn(x1, x2, gate, up, down):
    n = EXPERTS * SLOTS
    whole = pl.BlockSpec((n, D), lambda j: (0, 0))
    piece = pl.BlockSpec((1, D, 512), lambda j: (j, 0, 0))
    return pl.pallas_call(
        ffn_kernel,
        grid=(N_EXP,),
        in_specs=[whole, whole, piece, piece, piece],
        out_specs=[whole, whole],
        out_shape=[sds((n, D), F32), sds((n, D), BF)],
        scratch_shapes=[pltpu.VMEM((n, D), F32), pltpu.VMEM((n, D), F32)],
        compiler_params=pltpu.CompilerParams(vmem_limit_bytes=VMEM),
        cost_estimate=pl.CostEstimate(
            flops=2 * 2 * n * D * 2048 * 3, bytes_accessed=18 << 20, transcendentals=0
        ),
    )(x1, x2, gate, up, down)


def combine_kernel(ret_ref, didx_ref, gates_ref, sum_ref, out_ref):
    ret = ret_ref[...]
    total = sum_ref[...]
    for k in range(2):
        pick = hot(didx_ref[:, k : k + 1] == iota((FINE, EXPERTS * SLOTS), 1))
        total = total + gates_ref[:, k : k + 1] * dot(pick, ret)
    out_ref[...] = total.astype(BF)


def per_device(
    coarse_in,
    norm1_gain,
    qkv_weight,
    head_scale,
    out_weight,
    norm2_gain,
    mlp_in,
    mlp_out,
    fine_in,
    parent_device,
    parent_row,
    octant,
    octant_table,
    norm3_gain,
    expert_ids,
    expert_gates,
    gate_weight,
    up_weight,
    down_weight,
):
    s = lax.axis_index("seq")
    y = lax.axis_index("exp")
    gate = lax.all_gather(gate_weight, "exp", axis=0, tiled=True)
    up = lax.all_gather(up_weight, "exp", axis=0, tiled=True)
    down = lax.all_gather(down_weight, "exp", axis=0, tiled=True)

    pidx, didx, didxt, req = call(
        route_kernel,
        [
            sds((FINE, 1), jnp.int32),
            sds((FINE, 2), jnp.int32),
            sds((2, FINE), jnp.int32),
            sds((N_SEQ, PSLOTS, ROWS), BF),
        ],
        parent_device,
        parent_device.reshape(1, FINE),
        parent_row.reshape(FINE, 1),
        expert_ids,
        expert_ids.T,
    )
    feats = lax.all_gather(coarse_in, "exp", axis=0, tiled=False)
    q, kv = call(
        qkv_kernel,
        [sds((HEADS, ROWS, 2 * HD), BF), sds((N_SEQ, ROWS + PSLOTS, 2 * HD), BF)],
        feats,
        norm1_gain.reshape(1, D),
        qkv_weight,
        req,
    )
    q = lax.all_to_all(q, "seq", 0, 0, axis_index_groups=QUADS, tiled=True)
    kv = lax.all_to_all(kv, "seq", 0, 0, tiled=True)
    scale = lax.dynamic_slice(head_scale, (s % 4,), (1,)) * (math.log2(math.e) / math.sqrt(HD))
    att = call(
        attn_kernel, sds((HEADS, ROWS, HD), BF), scale.reshape(1, 1), q, kv, smem=(0,)
    )
    att = lax.all_to_all(att, "seq", 0, 0, axis_index_groups=QUADS, tiled=True)
    part = call(proj_kernel, sds((ROWS, D), BF), att, out_weight)
    parts = lax.all_to_all(part.reshape(N_EXP, 32, D), "exp", 0, 0, tiled=True)
    mixed, normed2 = call(
        mixed_kernel,
        [sds((32, D), F32), sds((32, D), BF)],
        y.astype(jnp.int32).reshape(1, 1),
        parts,
        feats,
        norm2_gain.reshape(1, D),
        smem=(0,),
    )
    normed2 = lax.all_gather(normed2, "exp", axis=0, tiled=True)
    part = call(mlp_kernel, sds((ROWS, D), BF), normed2, mlp_in, mlp_out)
    parts = lax.all_to_all(part.reshape(N_EXP, 32, D), "exp", 0, 0, tiled=True)
    rows = call(coarse_kernel, sds((32, D), BF), parts, mixed)
    coarse_new = lax.all_gather(rows, "exp", axis=0, tiled=True)
    served = call(serve_kernel, sds((N_SEQ * PSLOTS, D), BF), kv, coarse_new)
    served = lax.all_to_all(served, "seq", 0, 0, tiled=True)
    fine_sum, outgoing = call(
        fine_kernel,
        [sds((FINE, D), F32), sds((EXPERTS * SLOTS, D), BF)],
        served,
        pidx,
        fine_in,
        octant.reshape(FINE, 1),
        octant_table,
        norm3_gain.reshape(1, D),
        didxt,
    )
    mine = lax.all_to_all(outgoing, "seq", 0, 0, tiled=True)
    other = lax.ppermute(mine, "seq", SWAP)
    part_mine, part_other = ffn(mine, other, gate, up, down)
    from_other = lax.ppermute(part_other, "seq", SWAP)
    result = (part_mine + from_other.astype(F32)).astype(BF)
    returned = lax.all_to_all(result, "seq", 0, 0, tiled=True)
    fine_out = call(
        combine_kernel, sds((FINE, D), BF), returned, didx, expert_gates, fine_sum
    )
    return (coarse_new, fine_out)


def solution(mesh):
    return jax.shard_map(
        per_device,
        mesh=mesh,
        in_specs=(
            P("seq", "exp"),
            P(),
            P(None, None, "exp"),
            P("exp"),
            P("exp", None),
            P(),
            P(None, "exp"),
            P("exp", None),
            P(("seq", "exp"), None),
            P(("seq", "exp"), None),
            P(("seq", "exp")),
            P(("seq", "exp")),
            P(),
            P(),
            P(("seq", "exp"), None),
            P(("seq", "exp"), None),
            P("seq", None, "exp"),
            P("seq", None, "exp"),
            P("seq", None, "exp"),
        ),
        out_specs=(P("seq", None), P(("seq", "exp"), None)),
        check_vma=False,
    )
```

```python
import functools
import math

import jax
import jax.numpy as jnp
from jax import lax
from jax.experimental import pallas as pl
from jax.experimental.pallas import tpu as pltpu
from jax.sharding import PartitionSpec as P

EPSILON = 1e-06
BF = jnp.bfloat16
F32 = jnp.float32

N_SEQ = 32
N_EXP = 4
ROWS = 128
D = 1024
HEADS = 4
HD = 64
FINE = 160
EXPERTS = 16
SLOTS = 32
PSLOTS = 16
SIXTEENS = [[16 * a + b for b in range(16)] for a in range(8)]
SWAP = [(i, i ^ 1) for i in range(N_SEQ)]


def nbytes(x):
    return math.prod(x.shape) * x.dtype.itemsize


def call(kernel, out_shape, *args, smem=(), flops=0, spare=6, ready=(), **kw):
    space = [
        pl.BlockSpec(memory_space=pltpu.SMEM if i in smem else pltpu.VMEM) for i in range(len(args))
    ]
    outs = jax.tree.map(lambda _: pl.BlockSpec(memory_space=pltpu.VMEM), out_shape)
    moved = sum(nbytes(a) for a in args) + sum(nbytes(o) for o in jax.tree.leaves(out_shape))
    return pl.pallas_call(
        kernel,
        out_shape=out_shape,
        in_specs=space + [pl.BlockSpec(memory_space=pl.ANY)] * len(ready),
        out_specs=outs,
        compiler_params=pltpu.CompilerParams(vmem_limit_bytes=2 * moved + (spare << 20)),
        cost_estimate=pl.CostEstimate(flops=flops, bytes_accessed=1, transcendentals=0),
        **kw,
    )(*args, *ready)


def sds(shape, dtype):
    return jax.ShapeDtypeStruct(shape, dtype)


def dot(a, b):
    return jnp.dot(a, b, preferred_element_type=F32)


def dot_nt(a, b):
    return lax.dot_general(a, b, (((1,), (1,)), ((), ())), preferred_element_type=F32)


def iota(shape, dim):
    return lax.broadcasted_iota(jnp.int32, shape, dim)


def rms(x, gain):
    return x * lax.rsqrt(jnp.mean(x * x, axis=-1, keepdims=True) + EPSILON) * gain


def hot(cond):
    return jnp.where(cond, 1.0, 0.0).astype(BF)


def upright(row):
    n = row.shape[1]
    return jnp.sum(jnp.where(iota((n, n), 0) == iota((n, n), 1), row, jnp.zeros_like(row)), axis=1, keepdims=True)


def route_kernel(pdt_ref, prow_ref, idst_ref, pidx_ref, didx_ref, didxt_ref, req_ref):
    before = hot(iota((FINE, FINE), 0) < iota((FINE, FINE), 1))
    pdt = pdt_ref[...]
    member = hot(pdt == iota((N_SEQ, FINE), 0))
    rank = jnp.sum(member.astype(F32) * dot(member, before), axis=0, keepdims=True)
    pidxt = pdt.astype(F32) * PSLOTS + rank
    pidx_ref[...] = upright(pidxt).astype(jnp.int32)
    wanted = hot(pidxt == iota((N_SEQ * PSLOTS, FINE), 0).astype(F32))
    rows = jnp.broadcast_to(upright(prow_ref[...].astype(F32)), (FINE, ROWS)).astype(BF)
    req_ref[...] = dot(wanted, rows).astype(BF).reshape(N_SEQ, PSLOTS, ROWS)
    m = [hot(idst_ref[k : k + 1, :] == iota((EXPERTS, FINE), 0)) for k in range(2)]
    ahead = dot(m[0] + m[1], before)
    for k in range(2):
        r = jnp.sum(m[k].astype(F32) * ahead, axis=0, keepdims=True)
        slot = idst_ref[k : k + 1, :].astype(F32) * SLOTS + r
        didxt_ref[k : k + 1, :] = slot.astype(jnp.int32)
        didx_ref[:, k : k + 1] = upright(slot).astype(jnp.int32)


def around(y, k):
    return lax.rem(y - k + N_EXP, N_EXP)


def qkv_kernel(at_ref, f0_ref, f1_ref, f2_ref, f3_ref, gain_ref, w_ref, req_ref, x_ref, q0_ref, q1_ref, q2_ref, q3_ref, kv_ref, xs, qs):
    y, me = at_ref[0, 0], at_ref[0, 1]
    for k, f_ref in enumerate((f0_ref, f1_ref, f2_ref, f3_ref)):
        xs[around(y, k)] = f_ref[...]
    whole = jnp.concatenate([xs[c] for c in range(N_EXP)], axis=1)
    x_ref[...] = whole
    normed = rms(whole.astype(F32), gain_ref[...]).astype(BF)
    proj = [dot(normed, w_ref[i]) for i in range(3)]
    for h in range(HEADS):
        piece = [p[:, h * HD : (h + 1) * HD] for p in proj]
        q, k = [
            v * lax.rsqrt(jnp.mean(v * v, axis=-1, keepdims=True) + EPSILON) for v in piece[:2]
        ]
        qs[h] = jnp.concatenate([q, jnp.zeros_like(q)], axis=1).astype(BF)
        kv = jnp.concatenate([k, piece[2]], axis=1).astype(BF)
        for t in range(h, N_SEQ, HEADS):
            kv_ref[t, 0:ROWS, :] = kv
    kv_ref[:, ROWS : ROWS + PSLOTS, :] = req_ref[...]
    for k, q_ref in enumerate((q0_ref, q1_ref, q2_ref, q3_ref)):
        q_ref[...] = qs[me ^ k]


def attn_kernel(scale_ref, at_ref, q0_ref, q1_ref, q2_ref, q3_ref, kv_ref, out_ref):
    kv = kv_ref[:, 0:ROWS, :].reshape(N_SEQ * ROWS, 2 * HD)
    vones = jnp.where(iota(kv.shape, 1) < HD, jnp.ones_like(kv), kv)
    c = scale_ref[0, 0]
    me = at_ref[0, 1]
    for b, q_ref in enumerate((q0_ref, q1_ref, q2_ref, q3_ref)):
        s = dot_nt(q_ref[...], kv)
        top = jnp.max(s, axis=-1, keepdims=True)
        p = jnp.exp2((s - top) * c).astype(BF)
        o = dot(p, vones)
        o = o[:, HD:] / o[:, :HD]
        half = ROWS // 2
        packed = jnp.concatenate([o[:half], o[half:]], axis=1).astype(BF)
        for z in range(N_EXP):
            out_ref[(me ^ b) * N_EXP + z] = packed


def block_kernel(at_ref, att_ref, x_ref, gain_ref, wo_ref, win_ref, wout_ref, *rest):
    mixed_ref, part_ref, scr, wbuf, sem = rest[-5:]
    copies = [
        pltpu.make_async_copy(src, dst, sem.at[i])
        for i, (src, dst) in enumerate(
            (
                (wo_ref, wbuf.at[0]),
                (win_ref, wbuf.at[1]),
                (wout_ref, wbuf.at[2]),
            )
        )
    ]
    for c in copies:
        c.start()
    heads = []
    for z in range(N_EXP):
        for h in range(HEADS):
            a = att_ref[h * N_EXP + z]
            heads.append(jnp.concatenate([a[:, :HD], a[:, HD:]], axis=0))
    att = jnp.concatenate(heads, axis=1)
    copies[0].wait()
    mixed = x_ref[...].astype(F32) + dot(att, wbuf[0])
    for c in range(N_EXP):
        scr[c] = mixed[:, c * 256 : (c + 1) * 256]
    mixed_ref[...] = scr[at_ref[0, 0]]
    normed = rms(mixed, gain_ref[...]).astype(BF)
    copies[1].wait()
    inner = jax.nn.gelu(dot(normed, wbuf[1])).astype(BF)
    copies[2].wait()
    part = dot(inner, wbuf[2]).astype(BF)
    for c in range(N_EXP):
        part_ref[c] = part[:, c * 256 : (c + 1) * 256]


def block(at, att, x, gain, wo, win, wout, *ready):
    vm = pl.BlockSpec(memory_space=pltpu.VMEM)
    hbm = pl.BlockSpec(memory_space=pl.ANY)
    return pl.pallas_call(
        block_kernel,
        in_specs=[pl.BlockSpec(memory_space=pltpu.SMEM), vm, vm, vm] + [hbm] * (3 + len(ready)),
        out_specs=[vm, vm],
        out_shape=[sds((ROWS, 256), F32), sds((N_EXP, ROWS, 256), BF)],
        scratch_shapes=[
            pltpu.VMEM((N_EXP, ROWS, 256), F32),
            pltpu.VMEM((3, D, D), BF),
            pltpu.SemaphoreType.DMA((3,)),
        ],
        compiler_params=pltpu.CompilerParams(vmem_limit_bytes=58 << 20),
        cost_estimate=pl.CostEstimate(flops=1, bytes_accessed=1, transcendentals=0),
    )(at, att, x, gain, wo, win, wout, *ready)


def coarse_kernel(parts_ref, mixed_ref, out_ref):
    total = parts_ref[0].astype(F32)
    for c in range(1, N_EXP):
        total = total + parts_ref[c].astype(F32)
    out_ref[...] = (mixed_ref[...] + total).astype(BF)


def serve_kernel(at_ref, kv_ref, c0_ref, c1_ref, c2_ref, c3_ref, *rest):
    coarse_ref, out_ref, scr = rest[-3:]
    y = at_ref[0, 0]
    for k, c_ref in enumerate((c0_ref, c1_ref, c2_ref, c3_ref)):
        scr[around(y, k)] = c_ref[...]
    coarse = jnp.concatenate([scr[c] for c in range(N_EXP)], axis=1)
    coarse_ref[...] = coarse
    req = kv_ref[:, ROWS : ROWS + PSLOTS, :].reshape(N_SEQ * PSLOTS, ROWS)
    chosen = hot(req.astype(F32) == iota(req.shape, 1).astype(F32))
    out_ref[...] = dot(chosen, coarse).astype(BF)


def fine_kernel(rows_ref, pidx_ref, fine_ref, oct_ref, table_ref, gain_ref, didxt_ref, *rest):
    sum_ref, out_ref = rest[-2:]
    pick = hot(pidx_ref[...] == iota((FINE, N_SEQ * PSLOTS), 1))
    parents = dot(pick, rows_ref[...])
    octs = dot(hot(upright(oct_ref[...].astype(F32)) == iota((FINE, 8), 1).astype(F32)), table_ref[...])
    fine_sum = fine_ref[...].astype(F32) + parents + octs
    sum_ref[...] = fine_sum
    normed = rms(fine_sum, gain_ref[...]).astype(BF)
    slot = iota((EXPERTS * SLOTS, FINE), 0)
    place = hot((didxt_ref[0:1, :] == slot) | (didxt_ref[1:2, :] == slot))
    out_ref[...] = dot(place, normed).astype(BF)


def ffn_kernel(has_extra, at_ref, x_ref, extra_ref, gate_ref, u0, u1, u2, u3, d0, d1, d2, d3, out_ref, gb, ub, db, sem):
    y = at_ref[0, 0]
    ups, downs = (u0, u1, u2, u3), (d0, d1, d2, d3)
    copies = []
    for j, k in enumerate((0, 1, 3, 2)):
        places = ((gate_ref.at[around(y, k)], gb), (ups[j].at[0], ub), (downs[j].at[0], db))
        copies += [
            pltpu.make_async_copy(src, dst.at[j], sem.at[3 * j + i])
            for i, (src, dst) in enumerate(places)
        ]
    begun = 0

    def ready(i):
        nonlocal begun
        while begun < min(i + 4, len(copies)):
            copies[begun].start()
            begun += 1
        copies[i].wait()

    x = x_ref[...]
    acc = extra_ref[...].astype(F32) if has_extra else None
    for j in range(N_EXP):
        ready(3 * j)
        g = dot(x, gb[j])
        ready(3 * j + 1)
        u = dot(x, ub[j])
        act = (0.5 * g * (1.0 + jnp.tanh(0.5 * g)) * u).astype(BF)
        ready(3 * j + 2)
        part = dot_nt(act, db[j])
        acc = part if acc is None else acc + part
    out_ref[...] = acc.astype(BF)


def ffn(at, x, extra, gate, ups, downs):
    n = EXPERTS * SLOTS
    has_extra = extra is not None
    vm = pl.BlockSpec(memory_space=pltpu.VMEM)
    hbm = pl.BlockSpec(memory_space=pl.ANY)
    buf = pltpu.VMEM((N_EXP, D, 512), BF)
    return pl.pallas_call(
        functools.partial(ffn_kernel, has_extra),
        in_specs=[pl.BlockSpec(memory_space=pltpu.SMEM), vm, vm if has_extra else hbm] + [hbm] * 9,
        out_specs=vm,
        out_shape=sds((n, D), BF),
        scratch_shapes=[buf, buf, buf, pltpu.SemaphoreType.DMA((12,))],
        compiler_params=pltpu.CompilerParams(vmem_limit_bytes=54 << 20),
        cost_estimate=pl.CostEstimate(
            flops=2 * n * D * 2048 * 3, bytes_accessed=1 << 20, transcendentals=0
        ),
    )(at, x, extra if has_extra else x, gate, *ups, *downs)


def combine_kernel(ret_ref, didx_ref, gates_ref, sum_ref, out_ref):
    ret = ret_ref[...]
    total = sum_ref[...]
    for k in range(2):
        pick = hot(didx_ref[:, k : k + 1] == iota((FINE, EXPERTS * SLOTS), 1))
        total = total + upright(gates_ref[k : k + 1, :]) * dot(pick, ret)
    out_ref[...] = total.astype(BF)


def turn(v, k):
    return lax.ppermute(v, "exp", [(i, (i + k) % N_EXP) for i in range(N_EXP)])


def per_device(
    coarse_in,
    norm1_gain,
    qkv_weight,
    head_scale,
    out_weight,
    norm2_gain,
    mlp_in,
    mlp_out,
    fine_in,
    parent_device,
    parent_row,
    octant,
    octant_table,
    norm3_gain,
    expert_ids,
    expert_gates,
    gate_weight,
    up_weight,
    down_weight,
):
    s = lax.axis_index("seq")
    y = lax.axis_index("exp")
    at = jnp.stack([y, s % 4]).astype(jnp.int32).reshape(1, 2)
    feats = [coarse_in] + [turn(coarse_in, k) for k in (1, 2, 3)]
    wo = lax.all_gather(out_weight, "exp", axis=0, tiled=True)
    gate = lax.all_gather(gate_weight, "exp", axis=0, tiled=True)

    pidx, didx, didxt, req = call(
        route_kernel,
        [
            sds((FINE, 1), jnp.int32),
            sds((FINE, 2), jnp.int32),
            sds((2, FINE), jnp.int32),
            sds((N_SEQ, PSLOTS, ROWS), BF),
        ],
        parent_device.reshape(1, FINE),
        parent_row.reshape(1, FINE),
        expert_ids.T,
    )
    head_block = sds((ROWS, 2 * HD), BF)
    x, *qs, kv = call(
        qkv_kernel,
        [sds((ROWS, D), BF)] + [head_block] * 4 + [sds((N_SEQ, ROWS + PSLOTS, 2 * HD), BF)],
        at,
        *feats,
        norm1_gain.reshape(1, D),
        qkv_weight,
        req,
        smem=(0,),
        scratch_shapes=[pltpu.VMEM((N_EXP, ROWS, 256), BF), pltpu.VMEM((HEADS, ROWS, 2 * HD), BF)],
    )
    qs = [qs[0]] + [
        lax.ppermute(qs[k], "seq", [(i, i ^ k) for i in range(N_SEQ)]) for k in (1, 2, 3)
    ]
    kv = lax.all_to_all(kv, "seq", 0, 0, tiled=True)
    scale = lax.dynamic_slice(head_scale, (s % 4,), (1,)) * (math.log2(math.e) / math.sqrt(HD))
    att = call(
        attn_kernel,
        sds((16, ROWS // 2, 2 * HD), BF),
        scale.reshape(1, 1),
        at,
        *qs,
        kv,
        smem=(0, 1),
        spare=16,
    )
    att = lax.all_to_all(att, ("seq", "exp"), 0, 0, axis_index_groups=SIXTEENS, tiled=True)
    ur, ul = turn(up_weight, 1), turn(up_weight, 3)
    dr, dl = turn(down_weight, 1), turn(down_weight, 3)
    u2, d2 = turn(ur, 1), turn(dl, 3)
    mixed, part = block(
        at, att, x, norm2_gain.reshape(1, D), wo, mlp_in, mlp_out, dr, dl
    )
    parts = lax.all_to_all(part, "exp", 0, 0, tiled=True)
    piece = call(coarse_kernel, sds((ROWS, 256), BF), parts, mixed)
    pieces = [piece] + [turn(piece, k) for k in (1, 2, 3)]
    coarse_new, served = call(
        serve_kernel,
        [sds((ROWS, D), BF), sds((N_SEQ * PSLOTS, D), BF)],
        at,
        kv,
        *pieces,
        smem=(0,),
        scratch_shapes=[pltpu.VMEM((N_EXP, ROWS, 256), BF)],
    )
    served = lax.all_to_all(served, "seq", 0, 0, tiled=True)
    fine_sum, outgoing = call(
        fine_kernel,
        [sds((FINE, D), F32), sds((EXPERTS * SLOTS, D), BF)],
        served,
        pidx,
        fine_in,
        octant.reshape(1, FINE),
        octant_table,
        norm3_gain.reshape(1, D),
        didxt,
        ready=(ur, ul),
    )
    mine = lax.all_to_all(outgoing, "seq", 0, 0, tiled=True)
    other = lax.ppermute(mine, "seq", SWAP)
    ups = [up_weight, ur, ul, u2]
    downs = [down_weight, dr, dl, d2]
    for_other = ffn(at, other, None, gate, ups, downs)
    from_other = lax.ppermute(for_other, "seq", SWAP)
    result = ffn(at, mine, from_other, gate, ups, downs)
    returned = lax.all_to_all(result, "seq", 0, 0, tiled=True)
    fine_out = call(
        combine_kernel, sds((FINE, D), BF), returned, didx, expert_gates.T, fine_sum
    )
    return (coarse_new, fine_out)


def solution(mesh):
    return jax.shard_map(
        per_device,
        mesh=mesh,
        in_specs=(
            P("seq", "exp"),
            P(),
            P(None, None, "exp"),
            P("exp"),
            P("exp", None),
            P(),
            P(None, "exp"),
            P("exp", None),
            P(("seq", "exp"), None),
            P(("seq", "exp"), None),
            P(("seq", "exp")),
            P(("seq", "exp")),
            P(),
            P(),
            P(("seq", "exp"), None),
            P(("seq", "exp"), None),
            P("seq", None, "exp"),
            P("seq", None, "exp"),
            P("seq", None, "exp"),
        ),
        out_specs=(P("seq", None), P(("seq", "exp"), None)),
        check_vma=False,
    )
```

```python
import functools
import math

import jax
import jax.numpy as jnp
from jax import lax
from jax.experimental import pallas as pl
from jax.experimental.pallas import tpu as pltpu
from jax.sharding import PartitionSpec as P

EPSILON = 1e-06
BF = jnp.bfloat16
F32 = jnp.float32

N_SEQ = 32
N_EXP = 4
ROWS = 128
D = 1024
HEADS = 4
HD = 64
FINE = 160
EXPERTS = 16
SLOTS = 32
PSLOTS = 16
SIXTEENS = [[16 * a + b for b in range(16)] for a in range(8)]
SWAP = [(i, i ^ 1) for i in range(N_SEQ)]


def nbytes(x):
    return math.prod(x.shape) * x.dtype.itemsize


def call(kernel, out_shape, *args, smem=(), far=(), limit=60, flops=0, ready=(), **kw):
    space = [
        pl.BlockSpec(memory_space=pltpu.SMEM if i in smem else pltpu.VMEM) for i in range(len(args))
    ]
    outs = jax.tree.map(lambda _: pl.BlockSpec(memory_space=pltpu.VMEM), out_shape)
    for i in far:
        outs[i] = pl.BlockSpec(memory_space=pltpu.HBM)
    moved = sum(nbytes(a) for a in args) + sum(nbytes(o) for o in jax.tree.leaves(out_shape))
    return pl.pallas_call(
        kernel,
        out_shape=out_shape,
        in_specs=space + [pl.BlockSpec(memory_space=pl.ANY)] * len(ready),
        out_specs=outs,
        compiler_params=pltpu.CompilerParams(vmem_limit_bytes=limit << 20),
        cost_estimate=pl.CostEstimate(flops=flops, bytes_accessed=1, transcendentals=0),
        **kw,
    )(*args, *ready)


def sds(shape, dtype):
    return jax.ShapeDtypeStruct(shape, dtype)


def dot(a, b):
    return jnp.dot(a, b, preferred_element_type=F32)


def dot_nt(a, b):
    return lax.dot_general(a, b, (((1,), (1,)), ((), ())), preferred_element_type=F32)


def iota(shape, dim):
    return lax.broadcasted_iota(jnp.int32, shape, dim)


def rms(x, gain):
    return x * lax.rsqrt(jnp.mean(x * x, axis=-1, keepdims=True) + EPSILON) * gain


def hot(cond):
    return jnp.where(cond, 1.0, 0.0).astype(BF)


def upright(row):
    n = row.shape[1]
    return jnp.sum(jnp.where(iota((n, n), 0) == iota((n, n), 1), row, jnp.zeros_like(row)), axis=1, keepdims=True)


def route_kernel(pdt_ref, prow_ref, idst_ref, pidx_ref, didx_ref, didxt_ref, req_ref):
    before = hot(iota((FINE, FINE), 0) < iota((FINE, FINE), 1))
    pdt = pdt_ref[...]
    member = hot(pdt == iota((N_SEQ, FINE), 0))
    rank = jnp.sum(member.astype(F32) * dot(member, before), axis=0, keepdims=True)
    pidxt = pdt.astype(F32) * PSLOTS + rank
    pidx_ref[...] = upright(pidxt).astype(jnp.int32)
    wanted = hot(pidxt == iota((N_SEQ * PSLOTS, FINE), 0).astype(F32))
    rows = jnp.broadcast_to(upright(prow_ref[...].astype(F32)), (FINE, ROWS)).astype(BF)
    req_ref[...] = dot(wanted, rows).astype(BF).reshape(N_SEQ, PSLOTS, ROWS)
    m = [hot(idst_ref[k : k + 1, :] == iota((EXPERTS, FINE), 0)) for k in range(2)]
    ahead = dot(m[0] + m[1], before)
    for k in range(2):
        r = jnp.sum(m[k].astype(F32) * ahead, axis=0, keepdims=True)
        slot = idst_ref[k : k + 1, :].astype(F32) * SLOTS + r
        didxt_ref[k : k + 1, :] = slot.astype(jnp.int32)
        didx_ref[:, k : k + 1] = upright(slot).astype(jnp.int32)


def around(y, k):
    return lax.rem(y - k + N_EXP, N_EXP)


def qkv_kernel(at_ref, f0_ref, f1_ref, f2_ref, f3_ref, gain_ref, w_ref, req_ref, x_ref, q0_ref, q1_ref, q2_ref, q3_ref, kv_ref, xs, qs):
    y, me = at_ref[0, 0], at_ref[0, 1]
    for k, f_ref in enumerate((f0_ref, f1_ref, f2_ref, f3_ref)):
        xs[around(y, k)] = f_ref[...]
    whole = jnp.concatenate([xs[c] for c in range(N_EXP)], axis=1)
    x_ref[...] = whole
    normed = rms(whole.astype(F32), gain_ref[...]).astype(BF)
    proj = [dot(normed, w_ref[i]) for i in range(3)]
    for h in range(HEADS):
        piece = [p[:, h * HD : (h + 1) * HD] for p in proj]
        q, k = [
            v * lax.rsqrt(jnp.mean(v * v, axis=-1, keepdims=True) + EPSILON) for v in piece[:2]
        ]
        qs[h] = jnp.concatenate([q, jnp.zeros_like(q)], axis=1).astype(BF)
        kv = jnp.concatenate([k, piece[2]], axis=1).astype(BF)
        for t in range(h, N_SEQ, HEADS):
            kv_ref[t, 0:ROWS, :] = kv
    kv_ref[:, ROWS : ROWS + PSLOTS, :] = req_ref[...]
    for k, q_ref in enumerate((q0_ref, q1_ref, q2_ref, q3_ref)):
        q_ref[...] = qs[me ^ k]


def attn_kernel(scale_ref, at_ref, q0_ref, q1_ref, q2_ref, q3_ref, kv_ref, out_ref, req_ref):
    req_ref[...] = kv_ref[:, ROWS : ROWS + PSLOTS, :].reshape(N_SEQ * PSLOTS, ROWS)
    kv = kv_ref[:, 0:ROWS, :].reshape(N_SEQ * ROWS, 2 * HD)
    vones = jnp.where(iota(kv.shape, 1) < HD, jnp.ones_like(kv), kv)
    c = scale_ref[0, 0]
    me = at_ref[0, 1]
    for b, q_ref in enumerate((q0_ref, q1_ref, q2_ref, q3_ref)):
        s = dot_nt(q_ref[...], kv)
        top = jnp.max(s, axis=-1, keepdims=True)
        p = jnp.exp2((s - top) * c).astype(BF)
        o = dot(p, vones)
        o = o[:, HD:] / o[:, :HD]
        half = ROWS // 2
        packed = jnp.concatenate([o[:half], o[half:]], axis=1).astype(BF)
        for z in range(N_EXP):
            out_ref[(me ^ b) * N_EXP + z] = packed


def block_kernel(at_ref, att_ref, x_ref, gain_ref, wo_ref, win_ref, wout_ref, *rest):
    mixed_ref, part_ref, scr, wbuf, sem = rest[-5:]
    copies = [
        pltpu.make_async_copy(src, dst, sem.at[i])
        for i, (src, dst) in enumerate(
            (
                (wo_ref, wbuf.at[0]),
                (win_ref, wbuf.at[1]),
                (wout_ref, wbuf.at[2]),
            )
        )
    ]
    for c in copies:
        c.start()
    heads = []
    for z in range(N_EXP):
        for h in range(HEADS):
            a = att_ref[h * N_EXP + z]
            heads.append(jnp.concatenate([a[:, :HD], a[:, HD:]], axis=0))
    att = jnp.concatenate(heads, axis=1)
    copies[0].wait()
    mixed = x_ref[...].astype(F32) + dot(att, wbuf[0])
    for c in range(N_EXP):
        scr[c] = mixed[:, c * 256 : (c + 1) * 256]
    mixed_ref[...] = scr[at_ref[0, 0]]
    normed = rms(mixed, gain_ref[...]).astype(BF)
    copies[1].wait()
    inner = jax.nn.gelu(dot(normed, wbuf[1])).astype(BF)
    copies[2].wait()
    part = dot(inner, wbuf[2]).astype(BF)
    for c in range(N_EXP):
        part_ref[c] = part[:, c * 256 : (c + 1) * 256]


def block(at, att, x, gain, wo, win, wout, *ready):
    vm = pl.BlockSpec(memory_space=pltpu.VMEM)
    hbm = pl.BlockSpec(memory_space=pl.ANY)
    return pl.pallas_call(
        block_kernel,
        in_specs=[pl.BlockSpec(memory_space=pltpu.SMEM), vm, vm, vm] + [hbm] * (3 + len(ready)),
        out_specs=[vm, vm],
        out_shape=[sds((ROWS, 256), F32), sds((N_EXP, ROWS, 256), BF)],
        scratch_shapes=[
            pltpu.VMEM((N_EXP, ROWS, 256), F32),
            pltpu.VMEM((3, D, D), BF),
            pltpu.SemaphoreType.DMA((3,)),
        ],
        compiler_params=pltpu.CompilerParams(vmem_limit_bytes=58 << 20),
        cost_estimate=pl.CostEstimate(flops=1, bytes_accessed=1, transcendentals=0),
    )(at, att, x, gain, wo, win, wout, *ready)


def coarse_kernel(parts_ref, mixed_ref, out_ref):
    total = parts_ref[0].astype(F32)
    for c in range(1, N_EXP):
        total = total + parts_ref[c].astype(F32)
    out_ref[...] = (mixed_ref[...] + total).astype(BF)


def copy_out(out_ref, scr, sem, make):
    step = scr.shape[0] // 4
    copies = []
    for i in range(4):
        part = slice(i * step, (i + 1) * step)
        scr[part] = make(part)
        copies.append(pltpu.make_async_copy(scr.at[part], out_ref.at[part], sem.at[i]))
        copies[-1].start()
    for c in copies:
        c.wait()


def serve_kernel(at_ref, req_ref, c0_ref, c1_ref, c2_ref, c3_ref, coarse_ref, out_ref, cs, scr, sem):
    y = at_ref[0, 0]
    for k, c_ref in enumerate((c0_ref, c1_ref, c2_ref, c3_ref)):
        cs[around(y, k)] = c_ref[...]
    coarse = jnp.concatenate([cs[c] for c in range(N_EXP)], axis=1)
    coarse_ref[...] = coarse

    def make(part):
        req = req_ref[part].astype(F32)
        return dot(hot(req == iota(req.shape, 1).astype(F32)), coarse).astype(BF)

    copy_out(out_ref, scr, sem, make)


def fine_kernel(rows_ref, pidx_ref, fine_ref, oct_ref, table_ref, gain_ref, didxt_ref, *rest):
    sum_ref, out_ref, scr, sem = rest[-4:]
    pick = hot(pidx_ref[...] == iota((FINE, N_SEQ * PSLOTS), 1))
    parents = dot(pick, rows_ref[...])
    octs = dot(hot(upright(oct_ref[...].astype(F32)) == iota((FINE, 8), 1).astype(F32)), table_ref[...])
    fine_sum = fine_ref[...].astype(F32) + parents + octs
    sum_ref[...] = fine_sum
    normed = rms(fine_sum, gain_ref[...]).astype(BF)

    def make(part):
        slot = part.start + iota((part.stop - part.start, FINE), 0)
        place = hot((didxt_ref[0:1, :] == slot) | (didxt_ref[1:2, :] == slot))
        return dot(place, normed).astype(BF)

    copy_out(out_ref, scr, sem, make)


def stage_kernel(at_ref, gate_ref, u0_ref, d0_ref, d1_ref, d2_ref, g_ref, u_ref, d_ref, token_ref, sem):
    token_ref[...] = jnp.zeros_like(token_ref)
    y = at_ref[0, 0]
    copies = []
    for j, k in enumerate((0, 1, 3, 2)):
        copies.append((gate_ref.at[around(y, k)], g_ref.at[j]))
    copies.append((u0_ref.at[0], u_ref))
    for j, d in enumerate((d0_ref, d1_ref, d2_ref)):
        copies.append((d.at[0], d_ref.at[j]))
    copies = [pltpu.make_async_copy(src, dst, sem.at[i]) for i, (src, dst) in enumerate(copies)]
    for c in copies:
        c.start()
    for c in copies:
        c.wait()


HBM = pl.BlockSpec(memory_space=pltpu.HBM)
INNER = pl.BlockSpec(memory_space=pltpu.VMEM)
SCALAR = pl.BlockSpec(memory_space=pltpu.SMEM)


COST = pl.CostEstimate(flops=1, bytes_accessed=1, transcendentals=0)


def stage(at, gate, up, downs):
    return pl.pallas_call(
        stage_kernel,
        in_specs=[SCALAR] + [HBM] * 5,
        out_specs=[INNER] * 4,
        out_shape=[
            sds((4, D, 512), BF),
            sds((D, 512), BF),
            sds((3, D, 512), BF),
            sds((8, 128), F32),
        ],
        scratch_shapes=[pltpu.SemaphoreType.DMA((8,))],
        compiler_params=pltpu.CompilerParams(vmem_limit_bytes=53 << 20),
        cost_estimate=COST,
    )(at, gate, up, *downs)


def swiglu(x, gate, up, down):
    g = dot(x, gate)
    u = dot(x, up)
    return dot_nt((0.5 * g * (1.0 + jnp.tanh(0.5 * g)) * u).astype(BF), down)


def first_kernel(x_ref, g_ref, u_ref, d_ref, u1_ref, u2_ref, *rest):
    out_ref, ups, sem = rest[-3:]
    copies = [
        pltpu.make_async_copy(r.at[0], ups.at[j], sem.at[j]) for j, r in enumerate((u1_ref, u2_ref))
    ]
    for c in copies:
        c.start()
    x = x_ref[...]
    acc = swiglu(x, g_ref[0], u_ref[...], d_ref[0])
    for j in (1, 2):
        copies[j - 1].wait()
        acc = acc + swiglu(x, g_ref[j], ups[j - 1], d_ref[j])
    out_ref[...] = acc


def first(x, staged, ur, ul, *ready):
    n = EXPERTS * SLOTS
    return pl.pallas_call(
        first_kernel,
        in_specs=[INNER] * 4 + [HBM] * (2 + len(ready)),
        out_specs=[INNER] * 2,
        out_shape=[sds((n, D), F32), sds((2, D, 512), BF)],
        scratch_shapes=[pltpu.SemaphoreType.DMA((2,))],
        compiler_params=pltpu.CompilerParams(vmem_limit_bytes=30 << 20),
        cost_estimate=COST,
    )(x, *staged, ur, ul, *ready)


def second_kernel(x0_ref, x1_ref, x2_ref, x3_ref, g_ref, u_ref, d_ref, ups_ref, out_ref, x_out):
    x = jnp.concatenate([r[...] for r in (x0_ref, x1_ref, x2_ref, x3_ref)], axis=0)
    x_out[...] = x
    acc = swiglu(x, g_ref[0], u_ref[...], d_ref[0])
    for j in (1, 2):
        acc = acc + swiglu(x, g_ref[j], ups_ref[j - 1], d_ref[j])
    out_ref[...] = acc


def second(xs, staged, ups):
    n = EXPERTS * SLOTS
    return pl.pallas_call(
        second_kernel,
        in_specs=[INNER] * 8,
        out_specs=[INNER] * 2,
        out_shape=[sds((n, D), F32), sds((n, D), BF)],
        compiler_params=pltpu.CompilerParams(vmem_limit_bytes=30 << 20),
        cost_estimate=COST,
    )(*xs, *staged, ups)


def last_kernel(x_ref, acc_ref, g_ref, u_ref, d_ref, out_ref, u_out, d_out, sem):
    copies = [
        pltpu.make_async_copy(u_ref.at[0], u_out, sem.at[0]),
        pltpu.make_async_copy(d_ref.at[0], d_out, sem.at[1]),
    ]
    for c in copies:
        c.start()
    for c in copies:
        c.wait()
    out_ref[...] = (acc_ref[...] + swiglu(x_ref[...], g_ref[3], u_out[...], d_out[...])).astype(BF)


def last(x, acc, gate, up, down):
    n = EXPERTS * SLOTS
    return pl.pallas_call(
        last_kernel,
        in_specs=[INNER] * 3 + [HBM] * 2,
        out_specs=[INNER] * 3,
        out_shape=[sds((n, D), BF), sds((D, 512), BF), sds((D, 512), BF)],
        scratch_shapes=[pltpu.SemaphoreType.DMA((2,))],
        compiler_params=pltpu.CompilerParams(vmem_limit_bytes=30 << 20),
        cost_estimate=COST,
    )(x, acc, gate, up, down)


def final_kernel(x_ref, acc_ref, extra_ref, g_ref, u_ref, d_ref, out_ref):
    acc = acc_ref[...] + swiglu(x_ref[...], g_ref[3], u_ref[...], d_ref[...])
    out_ref[...] = (acc + extra_ref[...].astype(F32)).astype(BF)


def final(x, acc, extra, gate, up, down):
    n = EXPERTS * SLOTS
    return pl.pallas_call(
        final_kernel,
        in_specs=[INNER] * 6,
        out_specs=INNER,
        out_shape=sds((n, D), BF),
        compiler_params=pltpu.CompilerParams(vmem_limit_bytes=30 << 20),
        cost_estimate=COST,
    )(x, acc, extra, gate, up, down)


def combine_kernel(ret_ref, didx_ref, gates_ref, sum_ref, out_ref):
    ret = ret_ref[...]
    total = sum_ref[...]
    for k in range(2):
        pick = hot(didx_ref[:, k : k + 1] == iota((FINE, EXPERTS * SLOTS), 1))
        total = total + upright(gates_ref[k : k + 1, :]) * dot(pick, ret)
    out_ref[...] = total.astype(BF)


def turn(v, k):
    return lax.ppermute(v, "exp", [(i, (i + k) % N_EXP) for i in range(N_EXP)])


def per_device(
    coarse_in,
    norm1_gain,
    qkv_weight,
    head_scale,
    out_weight,
    norm2_gain,
    mlp_in,
    mlp_out,
    fine_in,
    parent_device,
    parent_row,
    octant,
    octant_table,
    norm3_gain,
    expert_ids,
    expert_gates,
    gate_weight,
    up_weight,
    down_weight,
):
    s = lax.axis_index("seq")
    y = lax.axis_index("exp")
    at = jnp.stack([y, s % 4]).astype(jnp.int32).reshape(1, 2)
    feats = [coarse_in] + [turn(coarse_in, k) for k in (1, 2, 3)]
    wo = lax.all_gather(out_weight, "exp", axis=0, tiled=True)
    gate = lax.all_gather(gate_weight, "exp", axis=0, tiled=True)

    pidx, didx, didxt, req = call(
        route_kernel,
        [
            sds((FINE, 1), jnp.int32),
            sds((FINE, 2), jnp.int32),
            sds((2, FINE), jnp.int32),
            sds((N_SEQ, PSLOTS, ROWS), BF),
        ],
        parent_device.reshape(1, FINE),
        parent_row.reshape(1, FINE),
        expert_ids.T,
    )
    head_block = sds((ROWS, 2 * HD), BF)
    x, *qs, kv = call(
        qkv_kernel,
        [sds((ROWS, D), BF)] + [head_block] * 4 + [sds((N_SEQ, ROWS + PSLOTS, 2 * HD), BF)],
        at,
        *feats,
        norm1_gain.reshape(1, D),
        qkv_weight,
        req,
        smem=(0,),
        scratch_shapes=[pltpu.VMEM((N_EXP, ROWS, 256), BF), pltpu.VMEM((HEADS, ROWS, 2 * HD), BF)],
    )
    qs = [qs[0]] + [
        lax.ppermute(qs[k], "seq", [(i, i ^ k) for i in range(N_SEQ)]) for k in (1, 2, 3)
    ]
    kv = lax.all_to_all(kv, "seq", 0, 0, tiled=True)
    scale = lax.dynamic_slice(head_scale, (s % 4,), (1,)) * (math.log2(math.e) / math.sqrt(HD))
    att, req = call(
        attn_kernel,
        [sds((16, ROWS // 2, 2 * HD), BF), sds((N_SEQ * PSLOTS, ROWS), BF)],
        scale.reshape(1, 1),
        at,
        *qs,
        kv,
        smem=(0, 1),
    )
    att = lax.all_to_all(att, ("seq", "exp"), 0, 0, axis_index_groups=SIXTEENS, tiled=True)
    ur, ul = turn(up_weight, 1), turn(up_weight, 3)
    dr, dl = turn(down_weight, 1), turn(down_weight, 3)
    u2, d2 = turn(ur, 1), turn(dl, 3)
    mixed, part = block(
        at, att, x, norm2_gain.reshape(1, D), wo, mlp_in, mlp_out, dr, dl
    )
    parts = lax.all_to_all(part, "exp", 0, 0, tiled=True)
    piece = call(coarse_kernel, sds((ROWS, 256), BF), parts, mixed)
    pieces = [piece] + [turn(piece, k) for k in (1, 2, 3)]
    coarse_new, served = call(
        serve_kernel,
        [sds((ROWS, D), BF), sds((N_SEQ * PSLOTS, D), BF)],
        at,
        req,
        *pieces,
        smem=(0,),
        far=(1,),
        scratch_shapes=[
            pltpu.VMEM((N_EXP, ROWS, 256), BF),
            pltpu.VMEM((N_SEQ * PSLOTS, D), BF),
            pltpu.SemaphoreType.DMA((4,)),
        ],
    )
    served = lax.all_to_all(served, "seq", 0, 0, tiled=True)
    *staged, token = stage(at, gate, up_weight, (down_weight, dr, dl))
    fine_sum, outgoing = call(
        fine_kernel,
        [sds((FINE, D), F32), sds((EXPERTS * SLOTS, D), BF)],
        served,
        pidx,
        fine_in,
        octant.reshape(1, FINE),
        octant_table,
        norm3_gain.reshape(1, D),
        didxt,
        ready=(ur, ul, token),
        limit=52,
        far=(1,),
        scratch_shapes=[
            pltpu.VMEM((EXPERTS * SLOTS, D), BF),
            pltpu.SemaphoreType.DMA((4,)),
        ],
    )
    mine = lax.all_to_all(outgoing, "seq", 0, 0, tiled=True)
    mine = mine.reshape(EXPERTS * SLOTS, D)
    others = [lax.ppermute(mine[i * 128 : i * 128 + 128], "seq", SWAP) for i in range(4)]
    acc_mine, ups = first(mine, staged, ur, ul)
    acc_other, other = second(others, staged, ups)
    for_other, u3, d3 = last(other, acc_other, staged[0], u2, d2)
    from_other = lax.ppermute(for_other, "seq", SWAP)
    result = final(mine, acc_mine, from_other, staged[0], u3, d3)
    returned = lax.all_to_all(result, "seq", 0, 0, tiled=True)
    fine_out = call(
        combine_kernel, sds((FINE, D), BF), returned, didx, expert_gates.T, fine_sum
    )
    return (coarse_new, fine_out)


def solution(mesh):
    return jax.shard_map(
        per_device,
        mesh=mesh,
        in_specs=(
            P("seq", "exp"),
            P(),
            P(None, None, "exp"),
            P("exp"),
            P("exp", None),
            P(),
            P(None, "exp"),
            P("exp", None),
            P(("seq", "exp"), None),
            P(("seq", "exp"), None),
            P(("seq", "exp")),
            P(("seq", "exp")),
            P(),
            P(),
            P(("seq", "exp"), None),
            P(("seq", "exp"), None),
            P("seq", None, "exp"),
            P("seq", None, "exp"),
            P("seq", None, "exp"),
        ),
        out_specs=(P("seq", None), P(("seq", "exp"), None)),
        check_vma=False,
    )
```

```python
import functools
import math

import jax
import jax.numpy as jnp
from jax import lax
from jax.experimental import pallas as pl
from jax.experimental.pallas import tpu as pltpu
from jax.sharding import PartitionSpec as P

EPSILON = 1e-06
BF = jnp.bfloat16
F32 = jnp.float32

N_SEQ = 32
N_EXP = 4
ROWS = 128
D = 1024
HEADS = 4
HD = 64
FINE = 160
EXPERTS = 16
SLOTS = 32
PSLOTS = 16
SIXTEENS = [[16 * a + b for b in range(16)] for a in range(8)]
SWAP = [(i, i ^ 1) for i in range(N_SEQ)]


def nbytes(x):
    return math.prod(x.shape) * x.dtype.itemsize


def call(kernel, out_shape, *args, smem=(), far=(), limit=60, flops=0, ready=(), **kw):
    space = [
        pl.BlockSpec(memory_space=pltpu.SMEM if i in smem else pltpu.VMEM) for i in range(len(args))
    ]
    outs = jax.tree.map(lambda _: pl.BlockSpec(memory_space=pltpu.VMEM), out_shape)
    for i in far:
        outs[i] = pl.BlockSpec(memory_space=pltpu.HBM)
    moved = sum(nbytes(a) for a in args) + sum(nbytes(o) for o in jax.tree.leaves(out_shape))
    return pl.pallas_call(
        kernel,
        out_shape=out_shape,
        in_specs=space + [pl.BlockSpec(memory_space=pl.ANY)] * len(ready),
        out_specs=outs,
        compiler_params=pltpu.CompilerParams(vmem_limit_bytes=limit << 20),
        cost_estimate=pl.CostEstimate(flops=flops, bytes_accessed=1, transcendentals=0),
        **kw,
    )(*args, *ready)


def sds(shape, dtype):
    return jax.ShapeDtypeStruct(shape, dtype)


def dot(a, b):
    return jnp.dot(a, b, preferred_element_type=F32)


def dot_nt(a, b):
    return lax.dot_general(a, b, (((1,), (1,)), ((), ())), preferred_element_type=F32)


def iota(shape, dim):
    return lax.broadcasted_iota(jnp.int32, shape, dim)


def rms(x, gain):
    return x * lax.rsqrt(jnp.mean(x * x, axis=-1, keepdims=True) + EPSILON) * gain


def hot(cond):
    return jnp.where(cond, 1.0, 0.0).astype(BF)


def upright(row):
    n = row.shape[1]
    return jnp.sum(jnp.where(iota((n, n), 0) == iota((n, n), 1), row, jnp.zeros_like(row)), axis=1, keepdims=True)


def route_kernel(pdt_ref, prow_ref, idst_ref, pidx_ref, didx_ref, didxt_ref, req_ref):
    before = hot(iota((FINE, FINE), 0) < iota((FINE, FINE), 1))
    pdt = pdt_ref[...]
    member = hot(pdt == iota((N_SEQ, FINE), 0))
    rank = jnp.sum(member.astype(F32) * dot(member, before), axis=0, keepdims=True)
    pidxt = pdt.astype(F32) * PSLOTS + rank
    pidx_ref[...] = upright(pidxt).astype(jnp.int32)
    wanted = hot(pidxt == iota((N_SEQ * PSLOTS, FINE), 0).astype(F32))
    rows = jnp.broadcast_to(upright(prow_ref[...].astype(F32)), (FINE, ROWS)).astype(BF)
    req_ref[...] = dot(wanted, rows).astype(BF).reshape(N_SEQ, PSLOTS, ROWS)
    m = [hot(idst_ref[k : k + 1, :] == iota((EXPERTS, FINE), 0)) for k in range(2)]
    ahead = dot(m[0] + m[1], before)
    for k in range(2):
        r = jnp.sum(m[k].astype(F32) * ahead, axis=0, keepdims=True)
        slot = idst_ref[k : k + 1, :].astype(F32) * SLOTS + r
        didxt_ref[k : k + 1, :] = slot.astype(jnp.int32)
        didx_ref[:, k : k + 1] = upright(slot).astype(jnp.int32)


def around(y, k):
    return lax.rem(y - k + N_EXP, N_EXP)


def qkv_kernel(at_ref, f0_ref, f1_ref, f2_ref, f3_ref, gain_ref, w_ref, req_ref, x_ref, q0_ref, q1_ref, q2_ref, q3_ref, kv_ref, xs, qs):
    y, me = at_ref[0, 0], at_ref[0, 1]
    for k, f_ref in enumerate((f0_ref, f1_ref, f2_ref, f3_ref)):
        xs[around(y, k)] = f_ref[...]
    whole = jnp.concatenate([xs[c] for c in range(N_EXP)], axis=1)
    x_ref[...] = whole
    normed = rms(whole.astype(F32), gain_ref[...]).astype(BF)
    proj = [dot(normed, w_ref[i]) for i in range(3)]
    for h in range(HEADS):
        piece = [p[:, h * HD : (h + 1) * HD] for p in proj]
        q, k = [
            v * lax.rsqrt(jnp.mean(v * v, axis=-1, keepdims=True) + EPSILON) for v in piece[:2]
        ]
        qs[h] = jnp.concatenate([q, jnp.zeros_like(q)], axis=1).astype(BF)
        kv = jnp.concatenate([k, piece[2]], axis=1).astype(BF)
        for t in range(h, N_SEQ, HEADS):
            kv_ref[t, 0:ROWS, :] = kv
    kv_ref[:, ROWS : ROWS + PSLOTS, :] = req_ref[...]
    for k, q_ref in enumerate((q0_ref, q1_ref, q2_ref, q3_ref)):
        q_ref[...] = qs[me ^ k]


def attn_kernel(scale_ref, at_ref, q0_ref, q1_ref, q2_ref, q3_ref, kv_ref, out_ref, req_ref):
    req_ref[...] = kv_ref[:, ROWS : ROWS + PSLOTS, :].reshape(N_SEQ * PSLOTS, ROWS)
    kv = kv_ref[:, 0:ROWS, :].reshape(N_SEQ * ROWS, 2 * HD)
    vones = jnp.where(iota(kv.shape, 1) < HD, jnp.ones_like(kv), kv)
    c = scale_ref[0, 0]
    me = at_ref[0, 1]
    for b, q_ref in enumerate((q0_ref, q1_ref, q2_ref, q3_ref)):
        s = dot_nt(q_ref[...], kv)
        top = jnp.max(s, axis=-1, keepdims=True)
        p = jnp.exp2((s - top) * c).astype(BF)
        o = dot(p, vones)
        o = o[:, HD:] / o[:, :HD]
        half = ROWS // 2
        packed = jnp.concatenate([o[:half], o[half:]], axis=1).astype(BF)
        for z in range(N_EXP):
            out_ref[(me ^ b) * N_EXP + z] = packed


def block_kernel(at_ref, att_ref, x_ref, gain_ref, wo_ref, win_ref, wout_ref, *rest):
    mixed_ref, p0_ref, p1_ref, p2_ref, p3_ref, scr, pieces, wbuf, sem = rest[-9:]
    copies = [
        pltpu.make_async_copy(src, dst, sem.at[i])
        for i, (src, dst) in enumerate(
            (
                (wo_ref, wbuf.at[0]),
                (win_ref, wbuf.at[1]),
                (wout_ref, wbuf.at[2]),
            )
        )
    ]
    for c in copies:
        c.start()
    heads = []
    for z in range(N_EXP):
        for h in range(HEADS):
            a = att_ref[h * N_EXP + z]
            heads.append(jnp.concatenate([a[:, :HD], a[:, HD:]], axis=0))
    att = jnp.concatenate(heads, axis=1)
    copies[0].wait()
    mixed = x_ref[...].astype(F32) + dot(att, wbuf[0])
    for c in range(N_EXP):
        scr[c] = mixed[:, c * 256 : (c + 1) * 256]
    mixed_ref[...] = scr[at_ref[0, 0]]
    normed = rms(mixed, gain_ref[...]).astype(BF)
    copies[1].wait()
    inner = jax.nn.gelu(dot(normed, wbuf[1])).astype(BF)
    copies[2].wait()
    part = dot(inner, wbuf[2]).astype(BF)
    for c in range(N_EXP):
        pieces[c] = part[:, c * 256 : (c + 1) * 256]
    for k, p_ref in enumerate((p0_ref, p1_ref, p2_ref, p3_ref)):
        p_ref[...] = pieces[lax.rem(at_ref[0, 0] + k, N_EXP)]


def block(at, att, x, gain, wo, win, wout, *ready):
    vm = pl.BlockSpec(memory_space=pltpu.VMEM)
    hbm = pl.BlockSpec(memory_space=pl.ANY)
    return pl.pallas_call(
        block_kernel,
        in_specs=[pl.BlockSpec(memory_space=pltpu.SMEM), vm, vm, vm] + [hbm] * (3 + len(ready)),
        out_specs=[vm] * 5,
        out_shape=[sds((ROWS, 256), F32)] + [sds((ROWS, 256), BF)] * 4,
        scratch_shapes=[
            pltpu.VMEM((N_EXP, ROWS, 256), F32),
            pltpu.VMEM((N_EXP, ROWS, 256), BF),
            pltpu.VMEM((3, D, D), BF),
            pltpu.SemaphoreType.DMA((3,)),
        ],
        compiler_params=pltpu.CompilerParams(vmem_limit_bytes=58 << 20),
        cost_estimate=pl.CostEstimate(flops=1, bytes_accessed=1, transcendentals=0),
    )(at, att, x, gain, wo, win, wout, *ready)


def coarse_kernel(p0_ref, p1_ref, p2_ref, p3_ref, mixed_ref, out_ref):
    total = p0_ref[...].astype(F32)
    for p_ref in (p1_ref, p2_ref, p3_ref):
        total = total + p_ref[...].astype(F32)
    out_ref[...] = (mixed_ref[...] + total).astype(BF)


def copy_out(out_ref, scr, sem, make):
    step = scr.shape[0] // 4
    copies = []
    for i in range(4):
        part = slice(i * step, (i + 1) * step)
        scr[part] = make(part)
        copies.append(pltpu.make_async_copy(scr.at[part], out_ref.at[part], sem.at[i]))
        copies[-1].start()
    for c in copies:
        c.wait()


def serve_kernel(at_ref, req_ref, c0_ref, c1_ref, c2_ref, c3_ref, coarse_ref, out_ref, cs, scr, sem):
    y = at_ref[0, 0]
    for k, c_ref in enumerate((c0_ref, c1_ref, c2_ref, c3_ref)):
        cs[around(y, k)] = c_ref[...]
    coarse = jnp.concatenate([cs[c] for c in range(N_EXP)], axis=1)
    coarse_ref[...] = coarse

    def make(part):
        req = req_ref[part].astype(F32)
        return dot(hot(req == iota(req.shape, 1).astype(F32)), coarse).astype(BF)

    copy_out(out_ref, scr, sem, make)


def fine_kernel(rows_ref, pidx_ref, fine_ref, oct_ref, table_ref, gain_ref, didxt_ref, *rest):
    sum_ref, out_ref, scr, sem = rest[-4:]
    pick = hot(pidx_ref[...] == iota((FINE, N_SEQ * PSLOTS), 1))
    parents = dot(pick, rows_ref[...])
    octs = dot(hot(upright(oct_ref[...].astype(F32)) == iota((FINE, 8), 1).astype(F32)), table_ref[...])
    fine_sum = fine_ref[...].astype(F32) + parents + octs
    sum_ref[...] = fine_sum
    normed = rms(fine_sum, gain_ref[...]).astype(BF)

    def make(part):
        slot = part.start + iota((part.stop - part.start, FINE), 0)
        place = hot((didxt_ref[0:1, :] == slot) | (didxt_ref[1:2, :] == slot))
        return dot(place, normed).astype(BF)

    copy_out(out_ref, scr, sem, make)


def stage_kernel(at_ref, gate_ref, u0_ref, d0_ref, d1_ref, d2_ref, g_ref, u_ref, d_ref, token_ref, sem):
    token_ref[...] = jnp.zeros_like(token_ref)
    y = at_ref[0, 0]
    copies = []
    for j, k in enumerate((0, 1, 3, 2)):
        copies.append((gate_ref.at[around(y, k)], g_ref.at[j]))
    copies.append((u0_ref.at[0], u_ref))
    for j, d in enumerate((d0_ref, d1_ref, d2_ref)):
        copies.append((d.at[0], d_ref.at[j]))
    copies = [pltpu.make_async_copy(src, dst, sem.at[i]) for i, (src, dst) in enumerate(copies)]
    for c in copies:
        c.start()
    for c in copies:
        c.wait()


HBM = pl.BlockSpec(memory_space=pltpu.HBM)
INNER = pl.BlockSpec(memory_space=pltpu.VMEM)
SCALAR = pl.BlockSpec(memory_space=pltpu.SMEM)


COST = pl.CostEstimate(flops=1, bytes_accessed=1, transcendentals=0)


def stage(at, gate, up, downs):
    return pl.pallas_call(
        stage_kernel,
        in_specs=[SCALAR] + [HBM] * 5,
        out_specs=[INNER] * 4,
        out_shape=[
            sds((4, D, 512), BF),
            sds((D, 512), BF),
            sds((3, D, 512), BF),
            sds((8, 128), F32),
        ],
        scratch_shapes=[pltpu.SemaphoreType.DMA((8,))],
        compiler_params=pltpu.CompilerParams(vmem_limit_bytes=53 << 20),
        cost_estimate=COST,
    )(at, gate, up, *downs)


def swiglu(x, gate, up, down):
    g = dot(x, gate)
    u = dot(x, up)
    return dot_nt((0.5 * g * (1.0 + jnp.tanh(0.5 * g)) * u).astype(BF), down)


def first_kernel(x_ref, g_ref, u_ref, d_ref, u1_ref, u2_ref, *rest):
    out_ref, ups, sem = rest[-3:]
    copies = [
        pltpu.make_async_copy(r.at[0], ups.at[j], sem.at[j]) for j, r in enumerate((u1_ref, u2_ref))
    ]
    for c in copies:
        c.start()
    x = x_ref[...]
    acc = swiglu(x, g_ref[0], u_ref[...], d_ref[0])
    for j in (1, 2):
        copies[j - 1].wait()
        acc = acc + swiglu(x, g_ref[j], ups[j - 1], d_ref[j])
    out_ref[...] = acc


def first(x, staged, ur, ul, *ready):
    n = EXPERTS * SLOTS
    return pl.pallas_call(
        first_kernel,
        in_specs=[INNER] * 4 + [HBM] * (2 + len(ready)),
        out_specs=[INNER] * 2,
        out_shape=[sds((n, D), F32), sds((2, D, 512), BF)],
        scratch_shapes=[pltpu.SemaphoreType.DMA((2,))],
        compiler_params=pltpu.CompilerParams(vmem_limit_bytes=30 << 20),
        cost_estimate=COST,
    )(x, *staged, ur, ul, *ready)


def second_kernel(x0_ref, x1_ref, x2_ref, x3_ref, g_ref, u_ref, d_ref, ups_ref, out_ref, x_out):
    x = jnp.concatenate([r[...] for r in (x0_ref, x1_ref, x2_ref, x3_ref)], axis=0)
    x_out[...] = x
    acc = swiglu(x, g_ref[0], u_ref[...], d_ref[0])
    for j in (1, 2):
        acc = acc + swiglu(x, g_ref[j], ups_ref[j - 1], d_ref[j])
    out_ref[...] = acc


def second(xs, staged, ups):
    n = EXPERTS * SLOTS
    return pl.pallas_call(
        second_kernel,
        in_specs=[INNER] * 8,
        out_specs=[INNER] * 2,
        out_shape=[sds((n, D), F32), sds((n, D), BF)],
        compiler_params=pltpu.CompilerParams(vmem_limit_bytes=30 << 20),
        cost_estimate=COST,
    )(*xs, *staged, ups)


def last_kernel(x_ref, acc_ref, g_ref, u_ref, d_ref, out_ref, u_out, d_out, sem):
    copies = [
        pltpu.make_async_copy(u_ref.at[0], u_out, sem.at[0]),
        pltpu.make_async_copy(d_ref.at[0], d_out, sem.at[1]),
    ]
    for c in copies:
        c.start()
    x = x_ref[...]
    g = dot(x, g_ref[3])
    copies[0].wait()
    u = dot(x, u_out[...])
    act = (0.5 * g * (1.0 + jnp.tanh(0.5 * g)) * u).astype(BF)
    copies[1].wait()
    out_ref[...] = (acc_ref[...] + dot_nt(act, d_out[...])).astype(BF)


def last(x, acc, gate, up, down):
    n = EXPERTS * SLOTS
    return pl.pallas_call(
        last_kernel,
        in_specs=[INNER] * 3 + [HBM] * 2,
        out_specs=[INNER] * 3,
        out_shape=[sds((n, D), BF), sds((D, 512), BF), sds((D, 512), BF)],
        scratch_shapes=[pltpu.SemaphoreType.DMA((2,))],
        compiler_params=pltpu.CompilerParams(vmem_limit_bytes=30 << 20),
        cost_estimate=COST,
    )(x, acc, gate, up, down)


def final_kernel(x_ref, acc_ref, extra_ref, g_ref, u_ref, d_ref, out_ref):
    acc = acc_ref[...] + swiglu(x_ref[...], g_ref[3], u_ref[...], d_ref[...])
    out_ref[...] = (acc + extra_ref[...].astype(F32)).astype(BF)


def final(x, acc, extra, gate, up, down):
    n = EXPERTS * SLOTS
    return pl.pallas_call(
        final_kernel,
        in_specs=[INNER] * 6,
        out_specs=INNER,
        out_shape=sds((n, D), BF),
        compiler_params=pltpu.CompilerParams(vmem_limit_bytes=30 << 20),
        cost_estimate=COST,
    )(x, acc, extra, gate, up, down)


def combine_kernel(ret_ref, didx_ref, gates_ref, sum_ref, out_ref):
    ret = ret_ref[...]
    total = sum_ref[...]
    for k in range(2):
        pick = hot(didx_ref[:, k : k + 1] == iota((FINE, EXPERTS * SLOTS), 1))
        total = total + upright(gates_ref[k : k + 1, :]) * dot(pick, ret)
    out_ref[...] = total.astype(BF)


def turn(v, k):
    return lax.ppermute(v, "exp", [(i, (i + k) % N_EXP) for i in range(N_EXP)])


def per_device(
    coarse_in,
    norm1_gain,
    qkv_weight,
    head_scale,
    out_weight,
    norm2_gain,
    mlp_in,
    mlp_out,
    fine_in,
    parent_device,
    parent_row,
    octant,
    octant_table,
    norm3_gain,
    expert_ids,
    expert_gates,
    gate_weight,
    up_weight,
    down_weight,
):
    s = lax.axis_index("seq")
    y = lax.axis_index("exp")
    at = jnp.stack([y, s % 4]).astype(jnp.int32).reshape(1, 2)
    feats = [coarse_in] + [turn(coarse_in, k) for k in (1, 2, 3)]
    wo = lax.all_gather(out_weight, "exp", axis=0, tiled=True)
    gate = lax.all_gather(gate_weight, "exp", axis=0, tiled=True)

    pidx, didx, didxt, req = call(
        route_kernel,
        [
            sds((FINE, 1), jnp.int32),
            sds((FINE, 2), jnp.int32),
            sds((2, FINE), jnp.int32),
            sds((N_SEQ, PSLOTS, ROWS), BF),
        ],
        parent_device.reshape(1, FINE),
        parent_row.reshape(1, FINE),
        expert_ids.T,
    )
    head_block = sds((ROWS, 2 * HD), BF)
    x, *qs, kv = call(
        qkv_kernel,
        [sds((ROWS, D), BF)] + [head_block] * 4 + [sds((N_SEQ, ROWS + PSLOTS, 2 * HD), BF)],
        at,
        *feats,
        norm1_gain.reshape(1, D),
        qkv_weight,
        req,
        smem=(0,),
        scratch_shapes=[pltpu.VMEM((N_EXP, ROWS, 256), BF), pltpu.VMEM((HEADS, ROWS, 2 * HD), BF)],
    )
    qs = [qs[0]] + [
        lax.ppermute(qs[k], "seq", [(i, i ^ k) for i in range(N_SEQ)]) for k in (1, 2, 3)
    ]
    kv = lax.all_to_all(kv, "seq", 0, 0, tiled=True)
    scale = lax.dynamic_slice(head_scale, (s % 4,), (1,)) * (math.log2(math.e) / math.sqrt(HD))
    att, req = call(
        attn_kernel,
        [sds((16, ROWS // 2, 2 * HD), BF), sds((N_SEQ * PSLOTS, ROWS), BF)],
        scale.reshape(1, 1),
        at,
        *qs,
        kv,
        smem=(0, 1),
        limit=24,
    )
    att = lax.all_to_all(att, ("seq", "exp"), 0, 0, axis_index_groups=SIXTEENS, tiled=True)
    ur, ul = turn(up_weight, 1), turn(up_weight, 3)
    dr, dl = turn(down_weight, 1), turn(down_weight, 3)
    u2, d2 = turn(ur, 1), turn(dl, 3)
    mixed, *parts = block(
        at, att, x, norm2_gain.reshape(1, D), wo, mlp_in, mlp_out, dr, dl
    )
    parts = [parts[0]] + [turn(parts[k], k) for k in (1, 2, 3)]
    piece = call(coarse_kernel, sds((ROWS, 256), BF), *parts, mixed, limit=8)
    pieces = [piece] + [turn(piece, k) for k in (1, 2, 3)]
    coarse_new, served = call(
        serve_kernel,
        [sds((ROWS, D), BF), sds((N_SEQ * PSLOTS, D), BF)],
        at,
        req,
        *pieces,
        smem=(0,),
        far=(1,),
        scratch_shapes=[
            pltpu.VMEM((N_EXP, ROWS, 256), BF),
            pltpu.VMEM((N_SEQ * PSLOTS, D), BF),
            pltpu.SemaphoreType.DMA((4,)),
        ],
    )
    served = lax.all_to_all(served, "seq", 0, 0, tiled=True)
    *staged, token = stage(at, gate, up_weight, (down_weight, dr, dl))
    fine_sum, outgoing = call(
        fine_kernel,
        [sds((FINE, D), F32), sds((EXPERTS * SLOTS, D), BF)],
        served,
        pidx,
        fine_in,
        octant.reshape(1, FINE),
        octant_table,
        norm3_gain.reshape(1, D),
        didxt,
        ready=(ur, ul, token),
        limit=60,
        far=(1,),
        scratch_shapes=[
            pltpu.VMEM((EXPERTS * SLOTS, D), BF),
            pltpu.SemaphoreType.DMA((4,)),
        ],
    )
    mine = lax.all_to_all(outgoing, "seq", 0, 0, tiled=True)
    mine = mine.reshape(EXPERTS * SLOTS, D)
    others = [lax.ppermute(mine[i * 128 : i * 128 + 128], "seq", SWAP) for i in range(4)]
    acc_mine, ups = first(mine, staged, ur, ul)
    acc_other, other = second(others, staged, ups)
    for_other, u3, d3 = last(other, acc_other, staged[0], u2, d2)
    from_other = lax.ppermute(for_other, "seq", SWAP)
    result = final(mine, acc_mine, from_other, staged[0], u3, d3)
    returned = lax.all_to_all(result, "seq", 0, 0, tiled=True)
    fine_out = call(
        combine_kernel, sds((FINE, D), BF), returned, didx, expert_gates.T, fine_sum, limit=12
    )
    return (coarse_new, fine_out)


def solution(mesh):
    return jax.shard_map(
        per_device,
        mesh=mesh,
        in_specs=(
            P("seq", "exp"),
            P(),
            P(None, None, "exp"),
            P("exp"),
            P("exp", None),
            P(),
            P(None, "exp"),
            P("exp", None),
            P(("seq", "exp"), None),
            P(("seq", "exp"), None),
            P(("seq", "exp")),
            P(("seq", "exp")),
            P(),
            P(),
            P(("seq", "exp"), None),
            P(("seq", "exp"), None),
            P("seq", None, "exp"),
            P("seq", None, "exp"),
            P("seq", None, "exp"),
        ),
        out_specs=(P("seq", None), P(("seq", "exp"), None)),
        check_vma=False,
    )
```

```python
import functools
import math

import jax
import jax.numpy as jnp
from jax import lax
from jax.experimental import pallas as pl
from jax.experimental.pallas import tpu as pltpu
from jax.sharding import PartitionSpec as P

EPSILON = 1e-06
BF = jnp.bfloat16
F32 = jnp.float32

N_SEQ = 32
N_EXP = 4
ROWS = 128
D = 1024
HEADS = 4
HD = 64
FINE = 160
EXPERTS = 16
SLOTS = 32
PSLOTS = 16
SIXTEENS = [[16 * a + b for b in range(16)] for a in range(8)]
SWAP = [(i, i ^ 1) for i in range(N_SEQ)]


def nbytes(x):
    return math.prod(x.shape) * x.dtype.itemsize


def call(kernel, out_shape, *args, smem=(), far=(), limit=60, flops=0, ready=(), **kw):
    space = [
        pl.BlockSpec(memory_space=pltpu.SMEM if i in smem else pltpu.VMEM) for i in range(len(args))
    ]
    outs = jax.tree.map(lambda _: pl.BlockSpec(memory_space=pltpu.VMEM), out_shape)
    for i in far:
        outs[i] = pl.BlockSpec(memory_space=pltpu.HBM)
    moved = sum(nbytes(a) for a in args) + sum(nbytes(o) for o in jax.tree.leaves(out_shape))
    return pl.pallas_call(
        kernel,
        out_shape=out_shape,
        in_specs=space + [pl.BlockSpec(memory_space=pl.ANY)] * len(ready),
        out_specs=outs,
        compiler_params=pltpu.CompilerParams(vmem_limit_bytes=limit << 20),
        cost_estimate=pl.CostEstimate(flops=flops, bytes_accessed=1, transcendentals=0),
        **kw,
    )(*args, *ready)


def sds(shape, dtype):
    return jax.ShapeDtypeStruct(shape, dtype)


def dot(a, b):
    return jnp.dot(a, b, preferred_element_type=F32)


def dot_nt(a, b):
    return lax.dot_general(a, b, (((1,), (1,)), ((), ())), preferred_element_type=F32)


def iota(shape, dim):
    return lax.broadcasted_iota(jnp.int32, shape, dim)


def rms(x, gain):
    return x * lax.rsqrt(jnp.mean(x * x, axis=-1, keepdims=True) + EPSILON) * gain


def hot(cond):
    return jnp.where(cond, 1.0, 0.0).astype(BF)


def upright(row):
    n = row.shape[1]
    return jnp.sum(jnp.where(iota((n, n), 0) == iota((n, n), 1), row, jnp.zeros_like(row)), axis=1, keepdims=True)


def route_kernel(pdt_ref, prow_ref, idst_ref, pidx_ref, didx_ref, didxt_ref, req_ref):
    before = hot(iota((FINE, FINE), 0) < iota((FINE, FINE), 1))
    pdt = pdt_ref[...]
    member = hot(pdt == iota((N_SEQ, FINE), 0))
    rank = jnp.sum(member.astype(F32) * dot(member, before), axis=0, keepdims=True)
    pidxt = pdt.astype(F32) * PSLOTS + rank
    pidx_ref[...] = upright(pidxt).astype(jnp.int32)
    wanted = hot(pidxt == iota((N_SEQ * PSLOTS, FINE), 0).astype(F32))
    rows = jnp.broadcast_to(upright(prow_ref[...].astype(F32)), (FINE, ROWS)).astype(BF)
    req_ref[...] = dot(wanted, rows).astype(BF).reshape(N_SEQ, PSLOTS, ROWS)
    m = [hot(idst_ref[k : k + 1, :] == iota((EXPERTS, FINE), 0)) for k in range(2)]
    ahead = dot(m[0] + m[1], before)
    for k in range(2):
        r = jnp.sum(m[k].astype(F32) * ahead, axis=0, keepdims=True)
        slot = idst_ref[k : k + 1, :].astype(F32) * SLOTS + r
        didxt_ref[k : k + 1, :] = slot.astype(jnp.int32)
        didx_ref[:, k : k + 1] = upright(slot).astype(jnp.int32)


def around(y, k):
    return lax.rem(y - k + N_EXP, N_EXP)


def qkv_kernel(f0_ref, f1_ref, f2_ref, f3_ref, gain_ref, w_ref, req_ref, x_ref, q0_ref, q1_ref, q2_ref, q3_ref, kv_ref, xs, qs):
    y, me = lax.axis_index("exp"), lax.rem(lax.axis_index("seq"), HEADS)
    for k, f_ref in enumerate((f0_ref, f1_ref, f2_ref, f3_ref)):
        xs[around(y, k)] = f_ref[...]
    whole = jnp.concatenate([xs[c] for c in range(N_EXP)], axis=1)
    x_ref[...] = whole
    normed = rms(whole.astype(F32), gain_ref[...]).astype(BF)
    proj = [dot(normed, w_ref[i]) for i in range(3)]
    for h in range(HEADS):
        piece = [p[:, h * HD : (h + 1) * HD] for p in proj]
        q, k = [
            v * lax.rsqrt(jnp.mean(v * v, axis=-1, keepdims=True) + EPSILON) for v in piece[:2]
        ]
        qs[h] = jnp.concatenate([q, jnp.zeros_like(q)], axis=1).astype(BF)
        kv = jnp.concatenate([k, piece[2]], axis=1).astype(BF)
        for t in range(h, N_SEQ, HEADS):
            kv_ref[t, 0:ROWS, :] = kv
    kv_ref[:, ROWS : ROWS + PSLOTS, :] = req_ref[...]
    for k, q_ref in enumerate((q0_ref, q1_ref, q2_ref, q3_ref)):
        q_ref[...] = qs[me ^ k]


def attn_kernel(scale_ref, q0_ref, q1_ref, q2_ref, q3_ref, kv_ref, out_ref, req_ref):
    req_ref[...] = kv_ref[:, ROWS : ROWS + PSLOTS, :].reshape(N_SEQ * PSLOTS, ROWS)
    kv = kv_ref[:, 0:ROWS, :].reshape(N_SEQ * ROWS, 2 * HD)
    vones = jnp.where(iota(kv.shape, 1) < HD, jnp.ones_like(kv), kv)
    me = lax.rem(lax.axis_index("seq"), HEADS)
    c = scale_ref[me] * (math.log2(math.e) / math.sqrt(HD))
    for b, q_ref in enumerate((q0_ref, q1_ref, q2_ref, q3_ref)):
        s = dot_nt(q_ref[...], kv)
        top = jnp.max(s, axis=-1, keepdims=True)
        p = jnp.exp2((s - top) * c).astype(BF)
        o = dot(p, vones)
        o = o[:, HD:] / o[:, :HD]
        half = ROWS // 2
        packed = jnp.concatenate([o[:half], o[half:]], axis=1).astype(BF)
        for z in range(N_EXP):
            out_ref[(me ^ b) * N_EXP + z] = packed


def block_kernel(att_ref, x_ref, gain_ref, wo_ref, win_ref, wout_ref, *rest):
    mixed_ref, p0_ref, p1_ref, p2_ref, p3_ref, scr, pieces, wbuf, sem = rest[-9:]
    copies = [
        pltpu.make_async_copy(src, dst, sem.at[i])
        for i, (src, dst) in enumerate(
            (
                (wo_ref, wbuf.at[0]),
                (win_ref, wbuf.at[1]),
                (wout_ref, wbuf.at[2]),
            )
        )
    ]
    for c in copies:
        c.start()
    heads = []
    for z in range(N_EXP):
        for h in range(HEADS):
            a = att_ref[h * N_EXP + z]
            heads.append(jnp.concatenate([a[:, :HD], a[:, HD:]], axis=0))
    att = jnp.concatenate(heads, axis=1)
    copies[0].wait()
    mixed = x_ref[...].astype(F32) + dot(att, wbuf[0])
    for c in range(N_EXP):
        scr[c] = mixed[:, c * 256 : (c + 1) * 256]
    y = lax.axis_index("exp")
    mixed_ref[...] = scr[y]
    normed = rms(mixed, gain_ref[...]).astype(BF)
    copies[1].wait()
    inner = jax.nn.gelu(dot(normed, wbuf[1])).astype(BF)
    copies[2].wait()
    part = dot(inner, wbuf[2]).astype(BF)
    for c in range(N_EXP):
        pieces[c] = part[:, c * 256 : (c + 1) * 256]
    for k, p_ref in enumerate((p0_ref, p1_ref, p2_ref, p3_ref)):
        p_ref[...] = pieces[lax.rem(y + k, N_EXP)]


def block(att, x, gain, wo, win, wout, *ready):
    vm = pl.BlockSpec(memory_space=pltpu.VMEM)
    hbm = pl.BlockSpec(memory_space=pl.ANY)
    return pl.pallas_call(
        block_kernel,
        in_specs=[vm, vm, vm] + [hbm] * (3 + len(ready)),
        out_specs=[vm] * 5,
        out_shape=[sds((ROWS, 256), F32)] + [sds((ROWS, 256), BF)] * 4,
        scratch_shapes=[
            pltpu.VMEM((N_EXP, ROWS, 256), F32),
            pltpu.VMEM((N_EXP, ROWS, 256), BF),
            pltpu.VMEM((3, D, D), BF),
            pltpu.SemaphoreType.DMA((3,)),
        ],
        compiler_params=pltpu.CompilerParams(vmem_limit_bytes=58 << 20),
        cost_estimate=pl.CostEstimate(flops=1, bytes_accessed=1, transcendentals=0),
    )(att, x, gain, wo, win, wout, *ready)


def coarse_kernel(p0_ref, p1_ref, p2_ref, p3_ref, mixed_ref, out_ref):
    total = p0_ref[...].astype(F32)
    for p_ref in (p1_ref, p2_ref, p3_ref):
        total = total + p_ref[...].astype(F32)
    out_ref[...] = (mixed_ref[...] + total).astype(BF)


def copy_out(out_ref, scr, sem, make):
    step = scr.shape[0] // 4
    copies = []
    for i in range(4):
        part = slice(i * step, (i + 1) * step)
        scr[part] = make(part)
        copies.append(pltpu.make_async_copy(scr.at[part], out_ref.at[part], sem.at[i]))
        copies[-1].start()
    for c in copies:
        c.wait()


def serve_kernel(req_ref, c0_ref, c1_ref, c2_ref, c3_ref, coarse_ref, out_ref, cs, scr, sem):
    y = lax.axis_index("exp")
    for k, c_ref in enumerate((c0_ref, c1_ref, c2_ref, c3_ref)):
        cs[around(y, k)] = c_ref[...]
    coarse = jnp.concatenate([cs[c] for c in range(N_EXP)], axis=1)
    coarse_ref[...] = coarse

    def make(part):
        req = req_ref[part].astype(F32)
        return dot(hot(req == iota(req.shape, 1).astype(F32)), coarse).astype(BF)

    copy_out(out_ref, scr, sem, make)


def fine_kernel(rows_ref, pidx_ref, fine_ref, oct_ref, table_ref, gain_ref, didxt_ref, *rest):
    sum_ref, out_ref, scr, sem = rest[-4:]
    pick = hot(pidx_ref[...] == iota((FINE, N_SEQ * PSLOTS), 1))
    parents = dot(pick, rows_ref[...])
    octs = dot(hot(upright(oct_ref[...].astype(F32)) == iota((FINE, 8), 1).astype(F32)), table_ref[...])
    fine_sum = fine_ref[...].astype(F32) + parents + octs
    sum_ref[...] = fine_sum
    normed = rms(fine_sum, gain_ref[...]).astype(BF)

    def make(part):
        slot = part.start + iota((part.stop - part.start, FINE), 0)
        place = hot((didxt_ref[0:1, :] == slot) | (didxt_ref[1:2, :] == slot))
        return dot(place, normed).astype(BF)

    copy_out(out_ref, scr, sem, make)


def stage_kernel(gate_ref, u0_ref, d0_ref, d1_ref, d2_ref, g_ref, u_ref, d_ref, token_ref, sem):
    token_ref[...] = jnp.zeros_like(token_ref)
    y = lax.axis_index("exp")
    copies = []
    for j, k in enumerate((0, 1, 3, 2)):
        copies.append((gate_ref.at[around(y, k)], g_ref.at[j]))
    copies.append((u0_ref.at[0], u_ref))
    for j, d in enumerate((d0_ref, d1_ref, d2_ref)):
        copies.append((d.at[0], d_ref.at[j]))
    copies = [pltpu.make_async_copy(src, dst, sem.at[i]) for i, (src, dst) in enumerate(copies)]
    for c in copies:
        c.start()
    for c in copies:
        c.wait()


HBM = pl.BlockSpec(memory_space=pltpu.HBM)
INNER = pl.BlockSpec(memory_space=pltpu.VMEM)


COST = pl.CostEstimate(flops=1, bytes_accessed=1, transcendentals=0)


def stage(gate, up, downs):
    return pl.pallas_call(
        stage_kernel,
        in_specs=[HBM] * 5,
        out_specs=[INNER] * 4,
        out_shape=[
            sds((4, D, 512), BF),
            sds((D, 512), BF),
            sds((3, D, 512), BF),
            sds((8, 128), F32),
        ],
        scratch_shapes=[pltpu.SemaphoreType.DMA((8,))],
        compiler_params=pltpu.CompilerParams(vmem_limit_bytes=53 << 20),
        cost_estimate=COST,
    )(gate, up, *downs)


def relay_kernel(src_ref, ready_ref, out_ref, sem):
    copy = pltpu.make_async_copy(src_ref, out_ref, sem.at[0])
    copy.start()
    copy.wait()


def relay(src, ready):
    return pl.pallas_call(
        relay_kernel,
        in_specs=[HBM] * 2,
        out_specs=INNER,
        out_shape=sds(src.shape, src.dtype),
        scratch_shapes=[pltpu.SemaphoreType.DMA((1,))],
        compiler_params=pltpu.CompilerParams(vmem_limit_bytes=60 << 20),
        cost_estimate=COST,
    )(src, ready)


def swiglu(x, gate, up, down):
    g = dot(x, gate)
    u = dot(x, up)
    return dot_nt((0.5 * g * (1.0 + jnp.tanh(0.5 * g)) * u).astype(BF), down)


def first_kernel(x_ref, g_ref, u_ref, d_ref, u1_ref, u2_ref, *rest):
    out_ref, ups, sem = rest[-3:]
    copies = [
        pltpu.make_async_copy(r.at[0], ups.at[j], sem.at[j]) for j, r in enumerate((u1_ref, u2_ref))
    ]
    for c in copies:
        c.start()
    x = x_ref[...]
    acc = swiglu(x, g_ref[0], u_ref[...], d_ref[0])
    for j in (1, 2):
        copies[j - 1].wait()
        acc = acc + swiglu(x, g_ref[j], ups[j - 1], d_ref[j])
    out_ref[...] = acc


def first(x, staged, ur, ul, *ready):
    n = EXPERTS * SLOTS
    return pl.pallas_call(
        first_kernel,
        in_specs=[INNER] * 4 + [HBM] * (2 + len(ready)),
        out_specs=[INNER] * 2,
        out_shape=[sds((n, D), F32), sds((2, D, 512), BF)],
        scratch_shapes=[pltpu.SemaphoreType.DMA((2,))],
        compiler_params=pltpu.CompilerParams(vmem_limit_bytes=30 << 20),
        cost_estimate=COST,
    )(x, *staged, ur, ul, *ready)


def second_kernel(x0_ref, x1_ref, x2_ref, x3_ref, g_ref, u_ref, d_ref, ups_ref, out_ref, x_out):
    x = jnp.concatenate([r[...] for r in (x0_ref, x1_ref, x2_ref, x3_ref)], axis=0)
    x_out[...] = x
    acc = swiglu(x, g_ref[0], u_ref[...], d_ref[0])
    for j in (1, 2):
        acc = acc + swiglu(x, g_ref[j], ups_ref[j - 1], d_ref[j])
    out_ref[...] = acc


def second(xs, staged, ups):
    n = EXPERTS * SLOTS
    return pl.pallas_call(
        second_kernel,
        in_specs=[INNER] * 8,
        out_specs=[INNER] * 2,
        out_shape=[sds((n, D), F32), sds((n, D), BF)],
        compiler_params=pltpu.CompilerParams(vmem_limit_bytes=30 << 20),
        cost_estimate=COST,
    )(*xs, *staged, ups)


def last_kernel(x_ref, acc_ref, g_ref, u_ref, d_ref, out_ref, u_out, d_out, sem):
    copies = [
        pltpu.make_async_copy(u_ref.at[0], u_out, sem.at[0]),
        pltpu.make_async_copy(d_ref.at[0], d_out, sem.at[1]),
    ]
    for c in copies:
        c.start()
    x = x_ref[...]
    g = dot(x, g_ref[3])
    copies[0].wait()
    u = dot(x, u_out[...])
    act = (0.5 * g * (1.0 + jnp.tanh(0.5 * g)) * u).astype(BF)
    copies[1].wait()
    out_ref[...] = (acc_ref[...] + dot_nt(act, d_out[...])).astype(BF)


def last(x, acc, gate, up, down):
    n = EXPERTS * SLOTS
    return pl.pallas_call(
        last_kernel,
        in_specs=[INNER] * 3 + [HBM] * 2,
        out_specs=[INNER] * 3,
        out_shape=[sds((n, D), BF), sds((D, 512), BF), sds((D, 512), BF)],
        scratch_shapes=[pltpu.SemaphoreType.DMA((2,))],
        compiler_params=pltpu.CompilerParams(vmem_limit_bytes=30 << 20),
        cost_estimate=COST,
    )(x, acc, gate, up, down)


def own_kernel(x_ref, acc_ref, g_ref, u_ref, d_ref, out_ref):
    out_ref[...] = acc_ref[...] + swiglu(x_ref[...], g_ref[3], u_ref[...], d_ref[...])


def own(x, acc, gate, up, down):
    n = EXPERTS * SLOTS
    return pl.pallas_call(
        own_kernel,
        in_specs=[INNER] * 5,
        out_specs=INNER,
        out_shape=sds((n, D), F32),
        compiler_params=pltpu.CompilerParams(vmem_limit_bytes=30 << 20),
        cost_estimate=COST,
    )(x, acc, gate, up, down)


def join_kernel(acc_ref, extra_ref, out_ref):
    out_ref[...] = (acc_ref[...] + extra_ref[...].astype(F32)).astype(BF)


def combine_kernel(ret_ref, didx_ref, gates_ref, sum_ref, out_ref):
    ret = ret_ref[...]
    total = sum_ref[...]
    for k in range(2):
        pick = hot(didx_ref[:, k : k + 1] == iota((FINE, EXPERTS * SLOTS), 1))
        total = total + upright(gates_ref[k : k + 1, :]) * dot(pick, ret)
    out_ref[...] = total.astype(BF)


def turn(v, k):
    return lax.ppermute(v, "exp", [(i, (i + k) % N_EXP) for i in range(N_EXP)])


def per_device(
    coarse_in,
    norm1_gain,
    qkv_weight,
    head_scale,
    out_weight,
    norm2_gain,
    mlp_in,
    mlp_out,
    fine_in,
    parent_device,
    parent_row,
    octant,
    octant_table,
    norm3_gain,
    expert_ids,
    expert_gates,
    gate_weight,
    up_weight,
    down_weight,
):
    feats = [coarse_in] + [turn(coarse_in, k) for k in (1, 2, 3)]
    wo = lax.all_gather(out_weight, "exp", axis=0, tiled=True)
    gate = lax.all_gather(gate_weight, "exp", axis=0, tiled=True)

    pidx, didx, didxt, req = call(
        route_kernel,
        [
            sds((FINE, 1), jnp.int32),
            sds((FINE, 2), jnp.int32),
            sds((2, FINE), jnp.int32),
            sds((N_SEQ, PSLOTS, ROWS), BF),
        ],
        parent_device.reshape(1, FINE),
        parent_row.reshape(1, FINE),
        expert_ids.T,
    )
    head_block = sds((ROWS, 2 * HD), BF)
    x, *qs, kv = call(
        qkv_kernel,
        [sds((ROWS, D), BF)] + [head_block] * 4 + [sds((N_SEQ, ROWS + PSLOTS, 2 * HD), BF)],
        *feats,
        norm1_gain.reshape(1, D),
        qkv_weight,
        req,
        scratch_shapes=[pltpu.VMEM((N_EXP, ROWS, 256), BF), pltpu.VMEM((HEADS, ROWS, 2 * HD), BF)],
    )
    qs = [qs[0]] + [
        lax.ppermute(qs[k], "seq", [(i, i ^ k) for i in range(N_SEQ)]) for k in (1, 2, 3)
    ]
    kv = lax.all_to_all(kv, "seq", 0, 0, tiled=True)
    att, req = call(
        attn_kernel,
        [sds((16, ROWS // 2, 2 * HD), BF), sds((N_SEQ * PSLOTS, ROWS), BF)],
        head_scale,
        *qs,
        kv,
        smem=(0,),
        limit=24,
    )
    att = lax.all_to_all(att, ("seq", "exp"), 0, 0, axis_index_groups=SIXTEENS, tiled=True)
    ur, ul = turn(up_weight, 1), turn(up_weight, 3)
    dr, dl = turn(down_weight, 1), turn(down_weight, 3)
    u2, d2 = turn(ur, 1), turn(relay(dl, ul), 3)
    mixed, *parts = block(
        att, x, norm2_gain.reshape(1, D), wo, mlp_in, mlp_out, dr, dl
    )
    parts = [parts[0]] + [turn(parts[k], k) for k in (1, 2, 3)]
    piece = call(coarse_kernel, sds((ROWS, 256), BF), *parts, mixed, limit=8)
    pieces = [piece] + [turn(piece, k) for k in (1, 2, 3)]
    coarse_new, served = call(
        serve_kernel,
        [sds((ROWS, D), BF), sds((N_SEQ * PSLOTS, D), BF)],
        req,
        *pieces,
        far=(1,),
        scratch_shapes=[
            pltpu.VMEM((N_EXP, ROWS, 256), BF),
            pltpu.VMEM((N_SEQ * PSLOTS, D), BF),
            pltpu.SemaphoreType.DMA((4,)),
        ],
    )
    served = lax.all_to_all(served, "seq", 0, 0, tiled=True)
    *staged, token = stage(gate, up_weight, (down_weight, dr, dl))
    fine_sum, outgoing = call(
        fine_kernel,
        [sds((FINE, D), F32), sds((EXPERTS * SLOTS, D), BF)],
        served,
        pidx,
        fine_in,
        octant.reshape(1, FINE),
        octant_table,
        norm3_gain.reshape(1, D),
        didxt,
        ready=(token,),
        limit=60,
        far=(1,),
        scratch_shapes=[
            pltpu.VMEM((EXPERTS * SLOTS, D), BF),
            pltpu.SemaphoreType.DMA((4,)),
        ],
    )
    mine = lax.all_to_all(outgoing, "seq", 0, 0, tiled=True)
    mine = mine.reshape(EXPERTS * SLOTS, D)
    others = [lax.ppermute(mine[i * 128 : i * 128 + 128], "seq", SWAP) for i in range(4)]
    acc_mine, ups = first(mine, staged, ur, ul)
    acc_other, other = second(others, staged, ups)
    for_other, u3, d3 = last(other, acc_other, staged[0], u2, d2)
    from_other = lax.ppermute(for_other, "seq", SWAP)
    acc_mine = own(mine, acc_mine, staged[0], u3, d3)
    result = call(join_kernel, sds((EXPERTS * SLOTS, D), BF), acc_mine, from_other, limit=24)
    returned = lax.all_to_all(result, "seq", 0, 0, tiled=True)
    fine_out = call(
        combine_kernel, sds((FINE, D), BF), returned, didx, expert_gates.T, fine_sum, limit=12
    )
    return (coarse_new, fine_out)


def solution(mesh):
    return jax.shard_map(
        per_device,
        mesh=mesh,
        in_specs=(
            P("seq", "exp"),
            P(),
            P(None, None, "exp"),
            P("exp"),
            P("exp", None),
            P(),
            P(None, "exp"),
            P("exp", None),
            P(("seq", "exp"), None),
            P(("seq", "exp"), None),
            P(("seq", "exp")),
            P(("seq", "exp")),
            P(),
            P(),
            P(("seq", "exp"), None),
            P(("seq", "exp"), None),
            P("seq", None, "exp"),
            P("seq", None, "exp"),
            P("seq", None, "exp"),
        ),
        out_specs=(P("seq", None), P(("seq", "exp"), None)),
        check_vma=False,
    )
```

```python
import functools
import math

import jax
import jax.numpy as jnp
from jax import lax
from jax.experimental import pallas as pl
from jax.experimental.pallas import tpu as pltpu
from jax.sharding import PartitionSpec as P

EPSILON = 1e-06
BF = jnp.bfloat16
F32 = jnp.float32

N_SEQ = 32
N_EXP = 4
ROWS = 128
D = 1024
HEADS = 4
HD = 64
FINE = 160
EXPERTS = 16
SLOTS = 32
PSLOTS = 16
SIXTEENS = [[16 * a + b for b in range(16)] for a in range(8)]
SWAP = [(i, i ^ 1) for i in range(N_SEQ)]


def nbytes(x):
    return math.prod(x.shape) * x.dtype.itemsize


def call(kernel, out_shape, *args, smem=(), far=(), limit=60, flops=0, ready=(), **kw):
    space = [
        pl.BlockSpec(memory_space=pltpu.SMEM if i in smem else pltpu.VMEM) for i in range(len(args))
    ]
    outs = jax.tree.map(lambda _: pl.BlockSpec(memory_space=pltpu.VMEM), out_shape)
    for i in far:
        outs[i] = pl.BlockSpec(memory_space=pltpu.HBM)
    moved = sum(nbytes(a) for a in args) + sum(nbytes(o) for o in jax.tree.leaves(out_shape))
    return pl.pallas_call(
        kernel,
        out_shape=out_shape,
        in_specs=space + [pl.BlockSpec(memory_space=pl.ANY)] * len(ready),
        out_specs=outs,
        compiler_params=pltpu.CompilerParams(vmem_limit_bytes=limit << 20),
        cost_estimate=pl.CostEstimate(flops=flops, bytes_accessed=1, transcendentals=0),
        **kw,
    )(*args, *ready)


def sds(shape, dtype):
    return jax.ShapeDtypeStruct(shape, dtype)


def dot(a, b):
    return jnp.dot(a, b, preferred_element_type=F32)


def dot_nt(a, b):
    return lax.dot_general(a, b, (((1,), (1,)), ((), ())), preferred_element_type=F32)


def iota(shape, dim):
    return lax.broadcasted_iota(jnp.int32, shape, dim)


def rms(x, gain):
    return x * lax.rsqrt(jnp.mean(x * x, axis=-1, keepdims=True) + EPSILON) * gain


def hot(cond):
    return jnp.where(cond, 1.0, 0.0).astype(BF)


def upright(row):
    n = row.shape[1]
    return jnp.sum(jnp.where(iota((n, n), 0) == iota((n, n), 1), row, jnp.zeros_like(row)), axis=1, keepdims=True)


def route_kernel(pdt_ref, prow_ref, idst_ref, pidx_ref, didx_ref, didxt_ref, req_ref):
    before = hot(iota((FINE, FINE), 0) < iota((FINE, FINE), 1))
    pdt = pdt_ref[...]
    member = hot(pdt == iota((N_SEQ, FINE), 0))
    rank = jnp.sum(member.astype(F32) * dot(member, before), axis=0, keepdims=True)
    pidxt = pdt.astype(F32) * PSLOTS + rank
    pidx_ref[...] = upright(pidxt).astype(jnp.int32)
    wanted = hot(pidxt == iota((N_SEQ * PSLOTS, FINE), 0).astype(F32))
    rows = jnp.broadcast_to(upright(prow_ref[...].astype(F32)), (FINE, ROWS)).astype(BF)
    req_ref[...] = dot(wanted, rows).astype(BF).reshape(N_SEQ, PSLOTS, ROWS)
    m = [hot(idst_ref[k : k + 1, :] == iota((EXPERTS, FINE), 0)) for k in range(2)]
    ahead = dot(m[0] + m[1], before)
    for k in range(2):
        r = jnp.sum(m[k].astype(F32) * ahead, axis=0, keepdims=True)
        slot = idst_ref[k : k + 1, :].astype(F32) * SLOTS + r
        didxt_ref[k : k + 1, :] = slot.astype(jnp.int32)
        didx_ref[:, k : k + 1] = upright(slot).astype(jnp.int32)


def around(y, k):
    return lax.rem(y - k + N_EXP, N_EXP)


def qkv_kernel(f0_ref, f1_ref, f2_ref, f3_ref, gain_ref, w_ref, req_ref, x_ref, q0_ref, q1_ref, q2_ref, q3_ref, kv_ref, xs, qs):
    y, me = lax.axis_index("exp"), lax.rem(lax.axis_index("seq"), HEADS)
    for k, f_ref in enumerate((f0_ref, f1_ref, f2_ref, f3_ref)):
        xs[around(y, k)] = f_ref[...]
    whole = jnp.concatenate([xs[c] for c in range(N_EXP)], axis=1)
    x_ref[...] = whole
    normed = rms(whole.astype(F32), gain_ref[...]).astype(BF)
    proj = [dot(normed, w_ref[i]) for i in range(3)]
    for h in range(HEADS):
        piece = [p[:, h * HD : (h + 1) * HD] for p in proj]
        q, k = [
            v * lax.rsqrt(jnp.mean(v * v, axis=-1, keepdims=True) + EPSILON) for v in piece[:2]
        ]
        qs[h] = jnp.concatenate([q, jnp.zeros_like(q)], axis=1).astype(BF)
        kv = jnp.concatenate([k, piece[2]], axis=1).astype(BF)
        for t in range(h, N_SEQ, HEADS):
            kv_ref[t, 0:ROWS, :] = kv
    kv_ref[:, ROWS : ROWS + PSLOTS, :] = req_ref[...]
    for k, q_ref in enumerate((q0_ref, q1_ref, q2_ref, q3_ref)):
        q_ref[...] = qs[me ^ k]


def attn_kernel(scale_ref, q0_ref, q1_ref, q2_ref, q3_ref, kv_ref, out_ref, req_ref):
    req_ref[...] = kv_ref[:, ROWS : ROWS + PSLOTS, :].reshape(N_SEQ * PSLOTS, ROWS)
    kv = kv_ref[:, 0:ROWS, :].reshape(N_SEQ * ROWS, 2 * HD)
    vones = jnp.where(iota(kv.shape, 1) < HD, jnp.ones_like(kv), kv)
    me = lax.rem(lax.axis_index("seq"), HEADS)
    c = scale_ref[me] * (math.log2(math.e) / math.sqrt(HD))
    for b, q_ref in enumerate((q0_ref, q1_ref, q2_ref, q3_ref)):
        s = dot_nt(q_ref[...], kv)
        top = jnp.max(s, axis=-1, keepdims=True)
        p = jnp.exp2((s - top) * c).astype(BF)
        o = dot(p, vones)
        o = o[:, HD:] / o[:, :HD]
        half = ROWS // 2
        packed = jnp.concatenate([o[:half], o[half:]], axis=1).astype(BF)
        for z in range(N_EXP):
            out_ref[(me ^ b) * N_EXP + z] = packed


def block_kernel(att_ref, x_ref, gain_ref, wo_ref, win_ref, wout_ref, *rest):
    mixed_ref, p0_ref, p1_ref, p2_ref, p3_ref, scr, pieces, wbuf, sem = rest[-9:]
    copies = [
        pltpu.make_async_copy(src, dst, sem.at[i])
        for i, (src, dst) in enumerate(
            (
                (wo_ref, wbuf.at[0]),
                (win_ref, wbuf.at[1]),
                (wout_ref, wbuf.at[2]),
            )
        )
    ]
    for c in copies:
        c.start()
    heads = []
    for z in range(N_EXP):
        for h in range(HEADS):
            a = att_ref[h * N_EXP + z]
            heads.append(jnp.concatenate([a[:, :HD], a[:, HD:]], axis=0))
    att = jnp.concatenate(heads, axis=1)
    copies[0].wait()
    mixed = x_ref[...].astype(F32) + dot(att, wbuf[0])
    for c in range(N_EXP):
        scr[c] = mixed[:, c * 256 : (c + 1) * 256]
    y = lax.axis_index("exp")
    mixed_ref[...] = scr[y]
    normed = rms(mixed, gain_ref[...]).astype(BF)
    copies[1].wait()
    inner = jax.nn.gelu(dot(normed, wbuf[1])).astype(BF)
    copies[2].wait()
    part = dot(inner, wbuf[2]).astype(BF)
    for c in range(N_EXP):
        pieces[c] = part[:, c * 256 : (c + 1) * 256]
    for k, p_ref in enumerate((p0_ref, p1_ref, p2_ref, p3_ref)):
        p_ref[...] = pieces[lax.rem(y + k, N_EXP)]


def block(att, x, gain, wo, win, wout, *ready):
    vm = pl.BlockSpec(memory_space=pltpu.VMEM)
    hbm = pl.BlockSpec(memory_space=pl.ANY)
    return pl.pallas_call(
        block_kernel,
        in_specs=[vm, vm, vm] + [hbm] * (3 + len(ready)),
        out_specs=[vm] * 5,
        out_shape=[sds((ROWS, 256), F32)] + [sds((ROWS, 256), BF)] * 4,
        scratch_shapes=[
            pltpu.VMEM((N_EXP, ROWS, 256), F32),
            pltpu.VMEM((N_EXP, ROWS, 256), BF),
            pltpu.VMEM((3, D, D), BF),
            pltpu.SemaphoreType.DMA((3,)),
        ],
        compiler_params=pltpu.CompilerParams(vmem_limit_bytes=58 << 20),
        cost_estimate=pl.CostEstimate(flops=1, bytes_accessed=1, transcendentals=0),
    )(att, x, gain, wo, win, wout, *ready)


def coarse_kernel(p0_ref, p1_ref, p2_ref, p3_ref, mixed_ref, out_ref):
    total = p0_ref[...].astype(F32)
    for p_ref in (p1_ref, p2_ref, p3_ref):
        total = total + p_ref[...].astype(F32)
    out_ref[...] = (mixed_ref[...] + total).astype(BF)


def copy_out(out_ref, scr, sem, make):
    step = scr.shape[0] // 4
    copies = []
    for i in range(4):
        part = slice(i * step, (i + 1) * step)
        scr[part] = make(part)
        copies.append(pltpu.make_async_copy(scr.at[part], out_ref.at[part], sem.at[i]))
        copies[-1].start()
    for c in copies:
        c.wait()


def serve_kernel(req_ref, c0_ref, c1_ref, c2_ref, c3_ref, coarse_ref, out_ref, cs, scr, sem):
    y = lax.axis_index("exp")
    for k, c_ref in enumerate((c0_ref, c1_ref, c2_ref, c3_ref)):
        cs[around(y, k)] = c_ref[...]
    coarse = jnp.concatenate([cs[c] for c in range(N_EXP)], axis=1)
    coarse_ref[...] = coarse

    def make(part):
        req = req_ref[part].astype(F32)
        return dot(hot(req == iota(req.shape, 1).astype(F32)), coarse).astype(BF)

    copy_out(out_ref, scr, sem, make)


def fine_kernel(rows_ref, pidx_ref, fine_ref, oct_ref, table_ref, gain_ref, didxt_ref, *rest):
    sum_ref, out_ref, scr, sem = rest[-4:]
    pick = hot(pidx_ref[...] == iota((FINE, N_SEQ * PSLOTS), 1))
    parents = dot(pick, rows_ref[...])
    octs = dot(hot(upright(oct_ref[...].astype(F32)) == iota((FINE, 8), 1).astype(F32)), table_ref[...])
    fine_sum = fine_ref[...].astype(F32) + parents + octs
    sum_ref[...] = fine_sum
    normed = rms(fine_sum, gain_ref[...]).astype(BF)

    def make(part):
        slot = part.start + iota((part.stop - part.start, FINE), 0)
        place = hot((didxt_ref[0:1, :] == slot) | (didxt_ref[1:2, :] == slot))
        return dot(place, normed).astype(BF)

    copy_out(out_ref, scr, sem, make)


def stage_kernel(gate_ref, u0_ref, d0_ref, d1_ref, d2_ref, g_ref, u_ref, d_ref, token_ref, sem):
    token_ref[...] = jnp.zeros_like(token_ref)
    y = lax.axis_index("exp")
    copies = []
    for j, k in enumerate((0, 1, 3, 2)):
        copies.append((gate_ref.at[around(y, k)], g_ref.at[j]))
    copies.append((u0_ref.at[0], u_ref))
    for j, d in enumerate((d0_ref, d1_ref, d2_ref)):
        copies.append((d.at[0], d_ref.at[j]))
    copies = [pltpu.make_async_copy(src, dst, sem.at[i]) for i, (src, dst) in enumerate(copies)]
    for c in copies:
        c.start()
    for c in copies:
        c.wait()


HBM = pl.BlockSpec(memory_space=pltpu.HBM)
INNER = pl.BlockSpec(memory_space=pltpu.VMEM)


COST = pl.CostEstimate(flops=1, bytes_accessed=1, transcendentals=0)


def stage(gate, up, downs):
    return pl.pallas_call(
        stage_kernel,
        in_specs=[HBM] * 5,
        out_specs=[INNER] * 4,
        out_shape=[
            sds((4, D, 512), BF),
            sds((D, 512), BF),
            sds((3, D, 512), BF),
            sds((8, 128), F32),
        ],
        scratch_shapes=[pltpu.SemaphoreType.DMA((8,))],
        compiler_params=pltpu.CompilerParams(vmem_limit_bytes=53 << 20),
        cost_estimate=COST,
    )(gate, up, *downs)


def relay_kernel(src_ref, ready_ref, out_ref, sem):
    copy = pltpu.make_async_copy(src_ref, out_ref, sem.at[0])
    copy.start()
    copy.wait()


def relay(src, ready):
    return pl.pallas_call(
        relay_kernel,
        in_specs=[HBM] * 2,
        out_specs=INNER,
        out_shape=sds(src.shape, src.dtype),
        scratch_shapes=[pltpu.SemaphoreType.DMA((1,))],
        compiler_params=pltpu.CompilerParams(vmem_limit_bytes=60 << 20),
        cost_estimate=COST,
    )(src, ready)


def swiglu(x, gate, up, down):
    g = dot(x, gate)
    u = dot(x, up)
    return dot_nt((0.5 * g * (1.0 + jnp.tanh(0.5 * g)) * u).astype(BF), down)


def first_kernel(x_ref, g_ref, u_ref, d_ref, u1_ref, u2_ref, *rest):
    out_ref, ups, sem = rest[-3:]
    copies = [
        pltpu.make_async_copy(r.at[0], ups.at[j], sem.at[j]) for j, r in enumerate((u1_ref, u2_ref))
    ]
    for c in copies:
        c.start()
    x = x_ref[...]
    acc = swiglu(x, g_ref[0], u_ref[...], d_ref[0])
    for j in (1, 2):
        copies[j - 1].wait()
        acc = acc + swiglu(x, g_ref[j], ups[j - 1], d_ref[j])
    out_ref[...] = acc


def first(x, staged, ur, ul, *ready):
    n = EXPERTS * SLOTS
    return pl.pallas_call(
        first_kernel,
        in_specs=[INNER] * 4 + [HBM] * (2 + len(ready)),
        out_specs=[INNER] * 2,
        out_shape=[sds((n, D), F32), sds((2, D, 512), BF)],
        scratch_shapes=[pltpu.SemaphoreType.DMA((2,))],
        compiler_params=pltpu.CompilerParams(vmem_limit_bytes=30 << 20),
        cost_estimate=COST,
    )(x, *staged, ur, ul, *ready)


def second_kernel(x0_ref, x1_ref, g_ref, u_ref, d_ref, ups_ref, out_ref, x_out):
    x = jnp.concatenate([r[...] for r in (x0_ref, x1_ref)], axis=0)
    x_out[...] = x
    acc = swiglu(x, g_ref[0], u_ref[...], d_ref[0])
    for j in (1, 2):
        acc = acc + swiglu(x, g_ref[j], ups_ref[j - 1], d_ref[j])
    out_ref[...] = acc


def second(xs, staged, ups):
    n = EXPERTS * SLOTS
    return pl.pallas_call(
        second_kernel,
        in_specs=[INNER] * 6,
        out_specs=[INNER] * 2,
        out_shape=[sds((n, D), F32), sds((n, D), BF)],
        compiler_params=pltpu.CompilerParams(vmem_limit_bytes=30 << 20),
        cost_estimate=COST,
    )(*xs, *staged, ups)


def last_kernel(x_ref, acc_ref, g_ref, u_ref, d_ref, out_ref, u_out, d_out, sem):
    copies = [
        pltpu.make_async_copy(u_ref.at[0], u_out, sem.at[0]),
        pltpu.make_async_copy(d_ref.at[0], d_out, sem.at[1]),
    ]
    for c in copies:
        c.start()
    x = x_ref[...]
    g = dot(x, g_ref[3])
    copies[0].wait()
    u = dot(x, u_out[...])
    act = (0.5 * g * (1.0 + jnp.tanh(0.5 * g)) * u).astype(BF)
    copies[1].wait()
    out_ref[...] = (acc_ref[...] + dot_nt(act, d_out[...])).astype(BF)


def last(x, acc, gate, up, down):
    n = EXPERTS * SLOTS
    return pl.pallas_call(
        last_kernel,
        in_specs=[INNER] * 3 + [HBM] * 2,
        out_specs=[INNER] * 3,
        out_shape=[sds((n, D), BF), sds((D, 512), BF), sds((D, 512), BF)],
        scratch_shapes=[pltpu.SemaphoreType.DMA((2,))],
        compiler_params=pltpu.CompilerParams(vmem_limit_bytes=30 << 20),
        cost_estimate=COST,
    )(x, acc, gate, up, down)


def own_kernel(x_ref, acc_ref, g_ref, u_ref, d_ref, out_ref):
    out_ref[...] = acc_ref[...] + swiglu(x_ref[...], g_ref[3], u_ref[...], d_ref[...])


def own(x, acc, gate, up, down):
    n = EXPERTS * SLOTS
    return pl.pallas_call(
        own_kernel,
        in_specs=[INNER] * 5,
        out_specs=INNER,
        out_shape=sds((n, D), F32),
        compiler_params=pltpu.CompilerParams(vmem_limit_bytes=30 << 20),
        cost_estimate=COST,
    )(x, acc, gate, up, down)


def join_kernel(acc_ref, extra_ref, out_ref):
    out_ref[...] = (acc_ref[...] + extra_ref[...].astype(F32)).astype(BF)


def combine_kernel(ret_ref, didx_ref, gates_ref, sum_ref, out_ref):
    ret = ret_ref[...]
    total = sum_ref[...]
    for k in range(2):
        pick = hot(didx_ref[:, k : k + 1] == iota((FINE, EXPERTS * SLOTS), 1))
        total = total + upright(gates_ref[k : k + 1, :]) * dot(pick, ret)
    out_ref[...] = total.astype(BF)


def turn(v, k):
    return lax.ppermute(v, "exp", [(i, (i + k) % N_EXP) for i in range(N_EXP)])


def per_device(
    coarse_in,
    norm1_gain,
    qkv_weight,
    head_scale,
    out_weight,
    norm2_gain,
    mlp_in,
    mlp_out,
    fine_in,
    parent_device,
    parent_row,
    octant,
    octant_table,
    norm3_gain,
    expert_ids,
    expert_gates,
    gate_weight,
    up_weight,
    down_weight,
):
    feats = [coarse_in] + [turn(coarse_in, k) for k in (1, 2, 3)]
    wo = lax.all_gather(out_weight, "exp", axis=0, tiled=True)
    gate = lax.all_gather(gate_weight, "exp", axis=0, tiled=True)

    pidx, didx, didxt, req = call(
        route_kernel,
        [
            sds((FINE, 1), jnp.int32),
            sds((FINE, 2), jnp.int32),
            sds((2, FINE), jnp.int32),
            sds((N_SEQ, PSLOTS, ROWS), BF),
        ],
        parent_device.reshape(1, FINE),
        parent_row.reshape(1, FINE),
        expert_ids.T,
    )
    head_block = sds((ROWS, 2 * HD), BF)
    x, *qs, kv = call(
        qkv_kernel,
        [sds((ROWS, D), BF)] + [head_block] * 4 + [sds((N_SEQ, ROWS + PSLOTS, 2 * HD), BF)],
        *feats,
        norm1_gain.reshape(1, D),
        qkv_weight,
        req,
        scratch_shapes=[pltpu.VMEM((N_EXP, ROWS, 256), BF), pltpu.VMEM((HEADS, ROWS, 2 * HD), BF)],
    )
    qs = [qs[0]] + [
        lax.ppermute(qs[k], "seq", [(i, i ^ k) for i in range(N_SEQ)]) for k in (1, 2, 3)
    ]
    kv = lax.all_to_all(kv, "seq", 0, 0, tiled=True)
    att, req = call(
        attn_kernel,
        [sds((16, ROWS // 2, 2 * HD), BF), sds((N_SEQ * PSLOTS, ROWS), BF)],
        head_scale,
        *qs,
        kv,
        smem=(0,),
        limit=24,
    )
    att = lax.all_to_all(att, ("seq", "exp"), 0, 0, axis_index_groups=SIXTEENS, tiled=True)
    ur, ul = turn(up_weight, 1), turn(up_weight, 3)
    dr, dl = turn(down_weight, 1), turn(down_weight, 3)
    u2, d2 = turn(ur, 1), turn(relay(dl, ul), 3)
    mixed, *parts = block(
        att, x, norm2_gain.reshape(1, D), wo, mlp_in, mlp_out, dr, dl
    )
    parts = [parts[0]] + [turn(parts[k], k) for k in (1, 2, 3)]
    piece = call(coarse_kernel, sds((ROWS, 256), BF), *parts, mixed, limit=8)
    pieces = [piece] + [turn(piece, k) for k in (1, 2, 3)]
    coarse_new, served = call(
        serve_kernel,
        [sds((ROWS, D), BF), sds((N_SEQ * PSLOTS, D), BF)],
        req,
        *pieces,
        far=(1,),
        scratch_shapes=[
            pltpu.VMEM((N_EXP, ROWS, 256), BF),
            pltpu.VMEM((N_SEQ * PSLOTS, D), BF),
            pltpu.SemaphoreType.DMA((4,)),
        ],
    )
    served = lax.all_to_all(served, "seq", 0, 0, tiled=True)
    *staged, token = stage(gate, up_weight, (down_weight, dr, dl))
    fine_sum, outgoing = call(
        fine_kernel,
        [sds((FINE, D), F32), sds((EXPERTS * SLOTS, D), BF)],
        served,
        pidx,
        fine_in,
        octant.reshape(1, FINE),
        octant_table,
        norm3_gain.reshape(1, D),
        didxt,
        ready=(token,),
        limit=56,
        far=(1,),
        scratch_shapes=[
            pltpu.VMEM((EXPERTS * SLOTS, D), BF),
            pltpu.SemaphoreType.DMA((4,)),
        ],
    )
    mine = lax.all_to_all(outgoing, "seq", 0, 0, tiled=True)
    mine = mine.reshape(EXPERTS * SLOTS, D)
    others = [lax.ppermute(mine[i * 256 : i * 256 + 256], "seq", SWAP) for i in range(2)]
    acc_mine, ups = first(mine, staged, ur, ul)
    acc_other, other = second(others, staged, ups)
    for_other, u3, d3 = last(other, acc_other, staged[0], u2, d2)
    from_other = lax.ppermute(for_other, "seq", SWAP)
    acc_mine = own(mine, acc_mine, staged[0], u3, d3)
    result = call(join_kernel, sds((EXPERTS * SLOTS, D), BF), acc_mine, from_other, limit=24)
    returned = lax.all_to_all(result, "seq", 0, 0, tiled=True)
    fine_out = call(
        combine_kernel, sds((FINE, D), BF), returned, didx, expert_gates.T, fine_sum, limit=12
    )
    return (coarse_new, fine_out)


def solution(mesh):
    return jax.shard_map(
        per_device,
        mesh=mesh,
        in_specs=(
            P("seq", "exp"),
            P(),
            P(None, None, "exp"),
            P("exp"),
            P("exp", None),
            P(),
            P(None, "exp"),
            P("exp", None),
            P(("seq", "exp"), None),
            P(("seq", "exp"), None),
            P(("seq", "exp")),
            P(("seq", "exp")),
            P(),
            P(),
            P(("seq", "exp"), None),
            P(("seq", "exp"), None),
            P("seq", None, "exp"),
            P("seq", None, "exp"),
            P("seq", None, "exp"),
        ),
        out_specs=(P("seq", None), P(("seq", "exp"), None)),
        check_vma=False,
    )
```

```python
import functools
import math

import jax
import jax.numpy as jnp
from jax import lax
from jax.experimental import pallas as pl
from jax.experimental.pallas import tpu as pltpu
from jax.sharding import PartitionSpec as P

EPSILON = 1e-06
BF = jnp.bfloat16
F32 = jnp.float32

N_SEQ = 32
N_EXP = 4
ROWS = 128
D = 1024
HEADS = 4
HD = 64
FINE = 160
EXPERTS = 16
SLOTS = 32
PSLOTS = 16
SIXTEENS = [[16 * a + b for b in range(16)] for a in range(8)]
SWAP = [(i, i ^ 1) for i in range(N_SEQ)]


def nbytes(x):
    return math.prod(x.shape) * x.dtype.itemsize


def call(kernel, out_shape, *args, smem=(), far=(), limit=60, flops=0, ready=(), **kw):
    space = [
        pl.BlockSpec(memory_space=pltpu.SMEM if i in smem else pltpu.VMEM) for i in range(len(args))
    ]
    outs = jax.tree.map(lambda _: pl.BlockSpec(memory_space=pltpu.VMEM), out_shape)
    for i in far:
        outs[i] = pl.BlockSpec(memory_space=pltpu.HBM)
    moved = sum(nbytes(a) for a in args) + sum(nbytes(o) for o in jax.tree.leaves(out_shape))
    return pl.pallas_call(
        kernel,
        out_shape=out_shape,
        in_specs=space + [pl.BlockSpec(memory_space=pl.ANY)] * len(ready),
        out_specs=outs,
        compiler_params=pltpu.CompilerParams(vmem_limit_bytes=limit << 20),
        cost_estimate=pl.CostEstimate(flops=flops, bytes_accessed=1, transcendentals=0),
        **kw,
    )(*args, *ready)


def sds(shape, dtype):
    return jax.ShapeDtypeStruct(shape, dtype)


def dot(a, b):
    return jnp.dot(a, b, preferred_element_type=F32)


def dot_nt(a, b):
    return lax.dot_general(a, b, (((1,), (1,)), ((), ())), preferred_element_type=F32)


def iota(shape, dim):
    return lax.broadcasted_iota(jnp.int32, shape, dim)


def rms(x, gain):
    return x * lax.rsqrt(jnp.mean(x * x, axis=-1, keepdims=True) + EPSILON) * gain


def hot(cond):
    return jnp.where(cond, 1.0, 0.0).astype(BF)


def upright(row):
    n = row.shape[1]
    return jnp.sum(jnp.where(iota((n, n), 0) == iota((n, n), 1), row, jnp.zeros_like(row)), axis=1, keepdims=True)


def route_kernel(pdt_ref, prow_ref, idst_ref, pidx_ref, didx_ref, didxt_ref, req_ref):
    before = hot(iota((FINE, FINE), 0) < iota((FINE, FINE), 1))
    pdt = pdt_ref[...]
    member = hot(pdt == iota((N_SEQ, FINE), 0))
    rank = jnp.sum(member.astype(F32) * dot(member, before), axis=0, keepdims=True)
    pidxt = pdt.astype(F32) * PSLOTS + rank
    pidx_ref[...] = upright(pidxt).astype(jnp.int32)
    wanted = hot(pidxt == iota((N_SEQ * PSLOTS, FINE), 0).astype(F32))
    rows = jnp.broadcast_to(upright(prow_ref[...].astype(F32)), (FINE, ROWS)).astype(BF)
    req_ref[...] = dot(wanted, rows).astype(BF).reshape(N_SEQ, PSLOTS, ROWS)
    m = [hot(idst_ref[k : k + 1, :] == iota((EXPERTS, FINE), 0)) for k in range(2)]
    ahead = dot(m[0] + m[1], before)
    for k in range(2):
        r = jnp.sum(m[k].astype(F32) * ahead, axis=0, keepdims=True)
        slot = idst_ref[k : k + 1, :].astype(F32) * SLOTS + r
        didxt_ref[k : k + 1, :] = slot.astype(jnp.int32)
        didx_ref[:, k : k + 1] = upright(slot).astype(jnp.int32)


def around(y, k):
    return lax.rem(y - k + N_EXP, N_EXP)


def qkv_kernel(f0_ref, f1_ref, f2_ref, f3_ref, gain_ref, w_ref, req_ref, x_ref, q0_ref, q1_ref, q2_ref, q3_ref, kv_ref, xs, qs):
    y, me = lax.axis_index("exp"), lax.rem(lax.axis_index("seq"), HEADS)
    for k, f_ref in enumerate((f0_ref, f1_ref, f2_ref, f3_ref)):
        xs[around(y, k)] = f_ref[...]
    whole = jnp.concatenate([xs[c] for c in range(N_EXP)], axis=1)
    x_ref[...] = whole
    normed = rms(whole.astype(F32), gain_ref[...]).astype(BF)
    proj = [dot(normed, w_ref[i]) for i in range(3)]
    for h in range(HEADS):
        piece = [p[:, h * HD : (h + 1) * HD] for p in proj]
        q, k = [
            v * lax.rsqrt(jnp.mean(v * v, axis=-1, keepdims=True) + EPSILON) for v in piece[:2]
        ]
        qs[h] = jnp.concatenate([q, jnp.zeros_like(q)], axis=1).astype(BF)
        kv = jnp.concatenate([k, piece[2]], axis=1).astype(BF)
        for t in range(h, N_SEQ, HEADS):
            kv_ref[t, 0:ROWS, :] = kv
    kv_ref[:, ROWS : ROWS + PSLOTS, :] = req_ref[...]
    for k, q_ref in enumerate((q0_ref, q1_ref, q2_ref, q3_ref)):
        q_ref[...] = qs[me ^ k]


def attn_kernel(scale_ref, q0_ref, q1_ref, q2_ref, q3_ref, kv_ref, out_ref, req_ref):
    req_ref[...] = kv_ref[:, ROWS : ROWS + PSLOTS, :].reshape(N_SEQ * PSLOTS, ROWS)
    kv = kv_ref[:, 0:ROWS, :].reshape(N_SEQ * ROWS, 2 * HD)
    vones = jnp.where(iota(kv.shape, 1) < HD, jnp.ones_like(kv), kv)
    me = lax.rem(lax.axis_index("seq"), HEADS)
    c = scale_ref[me] * (math.log2(math.e) / math.sqrt(HD))
    for b, q_ref in enumerate((q0_ref, q1_ref, q2_ref, q3_ref)):
        s = dot_nt(q_ref[...], kv)
        top = jnp.max(s, axis=-1, keepdims=True)
        p = jnp.exp2((s - top) * c).astype(BF)
        o = dot(p, vones)
        o = o[:, HD:] / o[:, :HD]
        half = ROWS // 2
        packed = jnp.concatenate([o[:half], o[half:]], axis=1).astype(BF)
        for z in range(N_EXP):
            out_ref[(me ^ b) * N_EXP + z] = packed


def block_kernel(att_ref, x_ref, gain_ref, wo_ref, win_ref, wout_ref, *rest):
    mixed_ref, p0_ref, p1_ref, p2_ref, p3_ref, scr, pieces, wbuf, sem = rest[-9:]
    copies = [
        pltpu.make_async_copy(src, dst, sem.at[i])
        for i, (src, dst) in enumerate(
            (
                (wo_ref, wbuf.at[0]),
                (win_ref, wbuf.at[1]),
                (wout_ref, wbuf.at[2]),
            )
        )
    ]
    for c in copies:
        c.start()
    heads = []
    for z in range(N_EXP):
        for h in range(HEADS):
            a = att_ref[h * N_EXP + z]
            heads.append(jnp.concatenate([a[:, :HD], a[:, HD:]], axis=0))
    att = jnp.concatenate(heads, axis=1)
    copies[0].wait()
    mixed = x_ref[...].astype(F32) + dot(att, wbuf[0])
    for c in range(N_EXP):
        scr[c] = mixed[:, c * 256 : (c + 1) * 256]
    y = lax.axis_index("exp")
    mixed_ref[...] = scr[y]
    normed = rms(mixed, gain_ref[...]).astype(BF)
    copies[1].wait()
    inner = jax.nn.gelu(dot(normed, wbuf[1])).astype(BF)
    copies[2].wait()
    part = dot(inner, wbuf[2]).astype(BF)
    for c in range(N_EXP):
        pieces[c] = part[:, c * 256 : (c + 1) * 256]
    for k, p_ref in enumerate((p0_ref, p1_ref, p2_ref, p3_ref)):
        p_ref[...] = pieces[lax.rem(y + k, N_EXP)]


def block(att, x, gain, wo, win, wout, *ready):
    vm = pl.BlockSpec(memory_space=pltpu.VMEM)
    hbm = pl.BlockSpec(memory_space=pl.ANY)
    return pl.pallas_call(
        block_kernel,
        in_specs=[vm, vm, vm] + [hbm] * (3 + len(ready)),
        out_specs=[vm] * 5,
        out_shape=[sds((ROWS, 256), F32)] + [sds((ROWS, 256), BF)] * 4,
        scratch_shapes=[
            pltpu.VMEM((N_EXP, ROWS, 256), F32),
            pltpu.VMEM((N_EXP, ROWS, 256), BF),
            pltpu.VMEM((3, D, D), BF),
            pltpu.SemaphoreType.DMA((3,)),
        ],
        compiler_params=pltpu.CompilerParams(vmem_limit_bytes=58 << 20),
        cost_estimate=pl.CostEstimate(flops=1, bytes_accessed=1, transcendentals=0),
    )(att, x, gain, wo, win, wout, *ready)


def coarse_kernel(p0_ref, p1_ref, p2_ref, p3_ref, mixed_ref, out_ref):
    total = p0_ref[...].astype(F32)
    for p_ref in (p1_ref, p2_ref, p3_ref):
        total = total + p_ref[...].astype(F32)
    out_ref[...] = (mixed_ref[...] + total).astype(BF)


def copy_out(out_ref, scr, sem, make):
    step = scr.shape[0] // 4
    copies = []
    for i in range(4):
        part = slice(i * step, (i + 1) * step)
        scr[part] = make(part)
        copies.append(pltpu.make_async_copy(scr.at[part], out_ref.at[part], sem.at[i]))
        copies[-1].start()
    for c in copies:
        c.wait()


def serve_kernel(req_ref, c0_ref, c1_ref, c2_ref, c3_ref, coarse_ref, out_ref, cs, scr, sem):
    y = lax.axis_index("exp")
    for k, c_ref in enumerate((c0_ref, c1_ref, c2_ref, c3_ref)):
        cs[around(y, k)] = c_ref[...]
    coarse = jnp.concatenate([cs[c] for c in range(N_EXP)], axis=1)
    coarse_ref[...] = coarse

    def make(part):
        req = req_ref[part].astype(F32)
        return dot(hot(req == iota(req.shape, 1).astype(F32)), coarse).astype(BF)

    copy_out(out_ref, scr, sem, make)


def fine_kernel(rows_ref, pidx_ref, fine_ref, oct_ref, table_ref, gain_ref, didxt_ref, *rest):
    sum_ref, out_ref, scr, sem = rest[-4:]
    pick = hot(pidx_ref[...] == iota((FINE, N_SEQ * PSLOTS), 1))
    parents = dot(pick, rows_ref[...])
    octs = dot(hot(upright(oct_ref[...].astype(F32)) == iota((FINE, 8), 1).astype(F32)), table_ref[...])
    fine_sum = fine_ref[...].astype(F32) + parents + octs
    sum_ref[...] = fine_sum
    normed = rms(fine_sum, gain_ref[...]).astype(BF)

    def make(part):
        slot = part.start + iota((part.stop - part.start, FINE), 0)
        place = hot((didxt_ref[0:1, :] == slot) | (didxt_ref[1:2, :] == slot))
        return dot(place, normed).astype(BF)

    copy_out(out_ref, scr, sem, make)


def stage_kernel(gate_ref, u0_ref, d0_ref, d1_ref, d2_ref, g_ref, u_ref, d_ref, token_ref, sem):
    token_ref[...] = jnp.zeros_like(token_ref)
    y = lax.axis_index("exp")
    copies = []
    for j, k in enumerate((0, 1, 3, 2)):
        copies.append((gate_ref.at[around(y, k)], g_ref.at[j]))
    copies.append((u0_ref.at[0], u_ref))
    for j, d in enumerate((d0_ref, d1_ref, d2_ref)):
        copies.append((d.at[0], d_ref.at[j]))
    copies = [pltpu.make_async_copy(src, dst, sem.at[i]) for i, (src, dst) in enumerate(copies)]
    for c in copies:
        c.start()
    for c in copies:
        c.wait()


HBM = pl.BlockSpec(memory_space=pltpu.HBM)
INNER = pl.BlockSpec(memory_space=pltpu.VMEM)


COST = pl.CostEstimate(flops=1, bytes_accessed=1, transcendentals=0)


def stage(gate, up, downs):
    return pl.pallas_call(
        stage_kernel,
        in_specs=[HBM] * 5,
        out_specs=[INNER] * 4,
        out_shape=[
            sds((4, D, 512), BF),
            sds((D, 512), BF),
            sds((3, D, 512), BF),
            sds((8, 128), F32),
        ],
        scratch_shapes=[pltpu.SemaphoreType.DMA((8,))],
        compiler_params=pltpu.CompilerParams(vmem_limit_bytes=53 << 20),
        cost_estimate=COST,
    )(gate, up, *downs)


def relay_kernel(src_ref, ready_ref, out_ref, sem):
    copy = pltpu.make_async_copy(src_ref, out_ref, sem.at[0])
    copy.start()
    copy.wait()


def relay(src, ready):
    return pl.pallas_call(
        relay_kernel,
        in_specs=[HBM] * 2,
        out_specs=INNER,
        out_shape=sds(src.shape, src.dtype),
        scratch_shapes=[pltpu.SemaphoreType.DMA((1,))],
        compiler_params=pltpu.CompilerParams(vmem_limit_bytes=60 << 20),
        cost_estimate=COST,
    )(src, ready)


def swiglu(x, gate, up, down):
    g = dot(x, gate)
    u = dot(x, up)
    return dot_nt((0.5 * g * (1.0 + jnp.tanh(0.5 * g)) * u).astype(BF), down)


def first_kernel(x_ref, g_ref, u_ref, d_ref, u1_ref, u2_ref, *rest):
    out_ref, ups, sem = rest[-3:]
    copies = [
        pltpu.make_async_copy(r.at[0], ups.at[j], sem.at[j]) for j, r in enumerate((u1_ref, u2_ref))
    ]
    for c in copies:
        c.start()
    x = x_ref[...]
    acc = swiglu(x, g_ref[0], u_ref[...], d_ref[0])
    for j in (1, 2):
        copies[j - 1].wait()
        acc = acc + swiglu(x, g_ref[j], ups[j - 1], d_ref[j])
    out_ref[...] = acc


def first(x, staged, ur, ul, *ready):
    n = EXPERTS * SLOTS
    return pl.pallas_call(
        first_kernel,
        in_specs=[INNER] * 4 + [HBM] * (2 + len(ready)),
        out_specs=[INNER] * 2,
        out_shape=[sds((n, D), F32), sds((2, D, 512), BF)],
        scratch_shapes=[pltpu.SemaphoreType.DMA((2,))],
        compiler_params=pltpu.CompilerParams(vmem_limit_bytes=30 << 20),
        cost_estimate=COST,
    )(x, *staged, ur, ul, *ready)


def second_kernel(x0_ref, x1_ref, g_ref, u_ref, d_ref, ups_ref, out_ref, x_out):
    x = jnp.concatenate([r[...] for r in (x0_ref, x1_ref)], axis=0)
    x_out[...] = x
    acc = swiglu(x, g_ref[0], u_ref[...], d_ref[0])
    for j in (1, 2):
        acc = acc + swiglu(x, g_ref[j], ups_ref[j - 1], d_ref[j])
    out_ref[...] = acc


def second(xs, staged, ups):
    n = EXPERTS * SLOTS
    return pl.pallas_call(
        second_kernel,
        in_specs=[INNER] * 6,
        out_specs=[INNER] * 2,
        out_shape=[sds((n, D), F32), sds((n, D), BF)],
        compiler_params=pltpu.CompilerParams(vmem_limit_bytes=30 << 20),
        cost_estimate=COST,
    )(*xs, *staged, ups)


def last_kernel(x_ref, acc_ref, g_ref, u_ref, d_ref, out_ref, u_out, d_out, sem):
    copies = [
        pltpu.make_async_copy(u_ref.at[0], u_out, sem.at[0]),
        pltpu.make_async_copy(d_ref.at[0], d_out, sem.at[1]),
    ]
    for c in copies:
        c.start()
    x = x_ref[...]
    g = dot(x, g_ref[3])
    copies[0].wait()
    u = dot(x, u_out[...])
    act = (0.5 * g * (1.0 + jnp.tanh(0.5 * g)) * u).astype(BF)
    copies[1].wait()
    out_ref[...] = (acc_ref[...] + dot_nt(act, d_out[...])).astype(BF)


def last(x, acc, gate, up, down):
    n = EXPERTS * SLOTS
    return pl.pallas_call(
        last_kernel,
        in_specs=[INNER] * 3 + [HBM] * 2,
        out_specs=[INNER] * 3,
        out_shape=[sds((n, D), BF), sds((D, 512), BF), sds((D, 512), BF)],
        scratch_shapes=[pltpu.SemaphoreType.DMA((2,))],
        compiler_params=pltpu.CompilerParams(vmem_limit_bytes=30 << 20),
        cost_estimate=COST,
    )(x, acc, gate, up, down)


def own_kernel(x_ref, acc_ref, g_ref, u_ref, d_ref, out_ref):
    out_ref[...] = acc_ref[...] + swiglu(x_ref[...], g_ref[3], u_ref[...], d_ref[...])


def own(x, acc, gate, up, down):
    n = EXPERTS * SLOTS
    return pl.pallas_call(
        own_kernel,
        in_specs=[INNER] * 5,
        out_specs=INNER,
        out_shape=sds((n, D), F32),
        compiler_params=pltpu.CompilerParams(vmem_limit_bytes=30 << 20),
        cost_estimate=COST,
    )(x, acc, gate, up, down)


def join_kernel(acc_ref, extra_ref, out_ref):
    out_ref[...] = (acc_ref[...] + extra_ref[...].astype(F32)).astype(BF)


def combine_kernel(ret_ref, didx_ref, gates_ref, sum_ref, out_ref):
    ret = ret_ref[...]
    total = sum_ref[...]
    for k in range(2):
        pick = hot(didx_ref[:, k : k + 1] == iota((FINE, EXPERTS * SLOTS), 1))
        total = total + upright(gates_ref[k : k + 1, :]) * dot(pick, ret)
    out_ref[...] = total.astype(BF)


def turn(v, k):
    return lax.ppermute(v, "exp", [(i, (i + k) % N_EXP) for i in range(N_EXP)])


def per_device(
    coarse_in,
    norm1_gain,
    qkv_weight,
    head_scale,
    out_weight,
    norm2_gain,
    mlp_in,
    mlp_out,
    fine_in,
    parent_device,
    parent_row,
    octant,
    octant_table,
    norm3_gain,
    expert_ids,
    expert_gates,
    gate_weight,
    up_weight,
    down_weight,
):
    feats = [coarse_in] + [turn(coarse_in, k) for k in (1, 2, 3)]
    wo = lax.all_gather(out_weight, "exp", axis=0, tiled=True)
    gate = lax.all_gather(gate_weight, "exp", axis=0, tiled=True)

    pidx, didx, didxt, req = call(
        route_kernel,
        [
            sds((FINE, 1), jnp.int32),
            sds((FINE, 2), jnp.int32),
            sds((2, FINE), jnp.int32),
            sds((N_SEQ, PSLOTS, ROWS), BF),
        ],
        parent_device.reshape(1, FINE),
        parent_row.reshape(1, FINE),
        expert_ids.T,
    )
    head_block = sds((ROWS, 2 * HD), BF)
    x, *qs, kv = call(
        qkv_kernel,
        [sds((ROWS, D), BF)] + [head_block] * 4 + [sds((N_SEQ, ROWS + PSLOTS, 2 * HD), BF)],
        *feats,
        norm1_gain.reshape(1, D),
        qkv_weight,
        req,
        scratch_shapes=[pltpu.VMEM((N_EXP, ROWS, 256), BF), pltpu.VMEM((HEADS, ROWS, 2 * HD), BF)],
    )
    qs = [qs[0]] + [
        lax.ppermute(qs[k], "seq", [(i, i ^ k) for i in range(N_SEQ)]) for k in (1, 2, 3)
    ]
    kv = lax.all_to_all(kv, "seq", 0, 0, tiled=True)
    att, req = call(
        attn_kernel,
        [sds((16, ROWS // 2, 2 * HD), BF), sds((N_SEQ * PSLOTS, ROWS), BF)],
        head_scale,
        *qs,
        kv,
        smem=(0,),
        limit=24,
    )
    att = lax.all_to_all(att, ("seq", "exp"), 0, 0, axis_index_groups=SIXTEENS, tiled=True)
    ur, ul = turn(up_weight, 1), turn(up_weight, 3)
    dr, dl = turn(down_weight, 1), turn(down_weight, 3)
    u2, d2 = turn(ur, 1), turn(relay(dl, ul), 3)
    mixed, *parts = block(
        att, x, norm2_gain.reshape(1, D), wo, mlp_in, mlp_out, dr, dl
    )
    parts = [parts[0]] + [turn(parts[k], k) for k in (1, 2, 3)]
    piece = call(coarse_kernel, sds((ROWS, 256), BF), *parts, mixed)
    pieces = [piece] + [turn(piece, k) for k in (1, 2, 3)]
    coarse_new, served = call(
        serve_kernel,
        [sds((ROWS, D), BF), sds((N_SEQ * PSLOTS, D), BF)],
        req,
        *pieces,
        far=(1,),
        scratch_shapes=[
            pltpu.VMEM((N_EXP, ROWS, 256), BF),
            pltpu.VMEM((N_SEQ * PSLOTS, D), BF),
            pltpu.SemaphoreType.DMA((4,)),
        ],
    )
    served = lax.all_to_all(served, "seq", 0, 0, tiled=True)
    *staged, token = stage(gate, up_weight, (down_weight, dr, dl))
    fine_sum, outgoing = call(
        fine_kernel,
        [sds((FINE, D), F32), sds((EXPERTS * SLOTS, D), BF)],
        served,
        pidx,
        fine_in,
        octant.reshape(1, FINE),
        octant_table,
        norm3_gain.reshape(1, D),
        didxt,
        ready=(token,),
        limit=52,
        far=(1,),
        scratch_shapes=[
            pltpu.VMEM((EXPERTS * SLOTS, D), BF),
            pltpu.SemaphoreType.DMA((4,)),
        ],
    )
    mine = lax.all_to_all(outgoing, "seq", 0, 0, tiled=True)
    mine = mine.reshape(EXPERTS * SLOTS, D)
    others = [lax.ppermute(mine[i * 256 : i * 256 + 256], "seq", SWAP) for i in range(2)]
    acc_mine, ups = first(mine, staged, ur, ul)
    acc_other, other = second(others, staged, ups)
    for_other, u3, d3 = last(other, acc_other, staged[0], u2, d2)
    from_other = lax.ppermute(for_other, "seq", SWAP)
    acc_mine = own(mine, acc_mine, staged[0], u3, d3)
    result = call(join_kernel, sds((EXPERTS * SLOTS, D), BF), acc_mine, from_other, limit=24)
    returned = lax.all_to_all(result, "seq", 0, 0, tiled=True)
    fine_out = call(
        combine_kernel, sds((FINE, D), BF), returned, didx, expert_gates.T, fine_sum, limit=12
    )
    return (coarse_new, fine_out)


def solution(mesh):
    return jax.shard_map(
        per_device,
        mesh=mesh,
        in_specs=(
            P("seq", "exp"),
            P(),
            P(None, None, "exp"),
            P("exp"),
            P("exp", None),
            P(),
            P(None, "exp"),
            P("exp", None),
            P(("seq", "exp"), None),
            P(("seq", "exp"), None),
            P(("seq", "exp")),
            P(("seq", "exp")),
            P(),
            P(),
            P(("seq", "exp"), None),
            P(("seq", "exp"), None),
            P("seq", None, "exp"),
            P("seq", None, "exp"),
            P("seq", None, "exp"),
        ),
        out_specs=(P("seq", None), P(("seq", "exp"), None)),
        check_vma=False,
    )
```
